128 devices in a mesh: ctx: 32 (over x, y, core), dp: 4 (over z).
Axes of the slice: x: 4, y: 4, z: 4, core: 2. Of those that a mesh axis runs over, the one named last changes fastest.
Arguments:
- queries: bfloat16 [4, 8192, 1024], P('dp', 'ctx'), may hold values from -128 to 128
- keys: bfloat16 [4, 8192, 1024], P('dp', 'ctx'), may hold values from -4 to 4
- values: bfloat16 [4, 8192, 1024], P('dp', 'ctx'), may hold values from -6 to 6
- w_out: bfloat16 [1024, 1024], replicated, may hold values from -0.1875 to 0.1875
- d_out: bfloat16 [4, 8192, 1024], P('dp', 'ctx'), may hold values from -6 to 6
- lengths: int32 [4, 96], P('dp'), may hold values from 1 to 1024, 8192 in all within a row
Outputs:
- output: bfloat16 [4, 8192, 1024], P('dp', 'ctx')
- d_queries: bfloat16 [4, 8192, 1024], P('dp', 'ctx')
- d_keys: bfloat16 [4, 8192, 1024], P('dp', 'ctx')
- d_values: bfloat16 [4, 8192, 1024], P('dp', 'ctx')
- d_w_out: float32 [1024, 1024], P(('ctx', 'dp'))
The draws below stay inside these ranges and needn't reach their ends.
Inputs may be any that keep to these rules, and one draw needn't show every extreme that they name: `lengths`: each row lists the documents of one pack in order; they sum to 8192 and the longest has exactly 1024 positions.
All inputs are finite; a program needn't handle non-finite values.
Results may differ from the reference program's by a relative error of at most 0.03.
Values may be sent and summed in bfloat16 or wider, within the bound.
No kernel may reach another device: no remote copies, remote signals or barrier semaphores. Data moves between devices by JAX's collectives and lax.ppermute only.
A program may use at most 128 MiB of HBM per device.

```python
import math
import jax
import jax.numpy as jnp
import numpy as np
from jax import lax

HEADS = 16
HDIM = 64
D = 1024
TOK_DEV = 256
SPAN = 4
TOKENS = 8192
PACKS = 4
NDOCS = 96
MAXDOC = 1024
N_CTX = 32


def shared_base(key):
    return jnp.clip(jax.random.normal(key, (PACKS, TOKENS, D), jnp.float32), -4.0, 4.0)


def draw_keys(key, part):
    base = shared_base(key)
    return base.astype(jnp.bfloat16)


def draw_queries(key, part):
    key = jax.random.fold_in(key, 5)
    own = jnp.clip(jax.random.normal(key, (PACKS, TOKENS, D), jnp.float32), -4.0, 4.0)
    return own.astype(jnp.bfloat16)


def level_of(key, shape, split, low, top_value):
    gain = 1.0
    for axis_at, blocks in split:
        steps = jax.random.uniform(jax.random.fold_in(jax.random.fold_in(key, 6), axis_at), (blocks,), jnp.float32, low / len(split), top_value / len(split))
        gain = gain * jnp.repeat(jnp.exp(steps), shape[axis_at] // blocks).reshape((-1,) + (1,) * (len(shape) - 1 - axis_at))
    return gain


def length_profile(number_of, total, limit, slope):
    portions = [(1 << 20) // math.isqrt(grade ** slope) + 1 for grade in range(2, number_of + 1)]
    spare, counts = total - limit - (number_of - 1), [1] * (number_of - 1)
    while spare > 0:
        free = [i for i in range(number_of - 1) if counts[i] < limit]
        pool, left = sum([portions[i] for i in free]), spare
        for i in free:
            more = min(limit - counts[i], max(1, left * portions[i] // pool), spare)
            counts[i] = counts[i] + more
            spare = spare - more
    return np.array([limit] + counts)


def uneven_parts(own_key, count, total, most, lean):
    if count == 2:
        one = jax.random.randint(own_key, (), max(1, total - most), min(most, total - 1) + 1)
        return jnp.stack([one, total - one])
    tallies = jnp.asarray(length_profile(count, total, most, lean), jnp.int32)
    twos = (count - 1) // 2
    giver, taker = tallies[1:1 + 2 * twos:2], tallies[2:2 + 2 * twos:2]
    room = jnp.minimum(giver - 1, most - taker)
    shifted = jax.random.randint(jax.random.fold_in(own_key, 1), (twos,), 0, 1 << 20) % (room + 1)
    tallies = tallies.at[1:1 + 2 * twos:2].set(giver - shifted).at[2:2 + 2 * twos:2].set(taker + shifted)
    return tallies[jax.random.permutation(jax.random.fold_in(own_key, 2), count)]


def scatter_about(rng, shape, width, reach, shards=(), held_as=jnp.bfloat16):
    factor_of = level_of(rng, shape, shards, -0.22, 0.18) if shards else 1.0
    entries = jax.random.normal(rng, shape, jnp.float32) * width * factor_of
    return jnp.minimum(jnp.maximum(entries, -reach), reach).astype(held_as)


def setup_inputs(seed: int = 0) -> dict:
    key_of = jax.random.split(jax.random.key(seed), 7)
    queries = draw_queries(jax.random.fold_in(key_of[6], 71), 0)
    keys = draw_keys(jax.random.fold_in(key_of[6], 71), 0)
    values = scatter_about(key_of[2], (PACKS, TOKENS, D), 1.0, 6.0, ((0, 4), (1, 32)))
    w_out = scatter_about(key_of[3], (D, D), D ** -0.5, 0.1875)
    d_out = scatter_about(key_of[4], (PACKS, TOKENS, D), 1.0, 6.0, ((0, 4), (1, 32)))
    lengths = jax.vmap(lambda own: uneven_parts(own, NDOCS, TOKENS, MAXDOC, 2))(jax.random.split(key_of[5], PACKS)).reshape((PACKS, NDOCS)).astype(jnp.int32)
    return {"queries": queries, "keys": keys, "values": values, "w_out": w_out, "d_out": d_out, "lengths": lengths}


def documents(positions, doc_ends):
    inside = (positions >= 0) & (positions < TOKENS)
    number = jnp.sum((doc_ends[None, :] <= positions[:, None]).astype(jnp.int32), axis=1)
    return jnp.where(inside, number, -1).astype(jnp.int32)


def rounded(values_in):
    return lax.optimization_barrier(values_in.astype(jnp.bfloat16)).astype(jnp.float32)


def one_pack(queries, keys, values, w_out, d_out, lengths):
    margin = SPAN * TOK_DEV
    window = (2 * SPAN + 1) * TOK_DEV
    doc_ends = jnp.cumsum(lengths).astype(jnp.int32)
    positions = jnp.arange(TOKENS + 2 * margin, dtype=jnp.int32) - margin
    all_docs = documents(positions, doc_ends)
    d_attn = jnp.dot(d_out, w_out.T, preferred_element_type=jnp.float32).astype(jnp.bfloat16)
    key_pad = jnp.pad(keys, ((margin, margin), (0, 0)))
    value_pad = jnp.pad(values, ((margin, margin), (0, 0)))

    def block(carry, index):
        key_acc, value_acc = carry
        begin = (index * TOK_DEV).astype(jnp.int32)
        query_block = lax.dynamic_slice_in_dim(queries, begin, TOK_DEV, 0).astype(jnp.float32).reshape(TOK_DEV, HEADS, HDIM)
        key_block = lax.dynamic_slice_in_dim(key_pad, begin, window, 0).astype(jnp.float32).reshape(window, HEADS, HDIM)
        value_block = lax.dynamic_slice_in_dim(value_pad, begin, window, 0).astype(jnp.float32).reshape(window, HEADS, HDIM)
        grad_block = lax.dynamic_slice_in_dim(d_attn, begin, TOK_DEV, 0).astype(jnp.float32).reshape(TOK_DEV, HEADS, HDIM)
        query_docs = lax.dynamic_slice_in_dim(all_docs, begin + margin, TOK_DEV, 0)
        key_docs = lax.dynamic_slice_in_dim(all_docs, begin, window, 0)
        same_doc = query_docs[:, None] == key_docs[None, :]
        scores = jnp.einsum("qhd,khd->hqk", query_block, key_block) * 0.125
        scores = jnp.where(same_doc[None], scores, -jnp.inf)
        row_max = jnp.max(scores, axis=2)
        exp_scores = jnp.exp(scores - row_max[:, :, None])
        row_total = jnp.sum(exp_scores, axis=2)
        attn_heads = jnp.einsum("hqk,khd->hqd", rounded(exp_scores), value_block) / row_total[:, :, None]
        attn = jnp.transpose(attn_heads, (1, 0, 2)).reshape(TOK_DEV, D).astype(jnp.bfloat16)
        log_total = row_max + jnp.log(row_total)
        attn_f = attn.astype(jnp.float32).reshape(TOK_DEV, HEADS, HDIM)
        delta = jnp.einsum("qhd,qhd->hq", attn_f, grad_block)
        likely = jnp.exp(scores - log_total[:, :, None])
        value_part = jnp.einsum("hqk,qhd->khd", rounded(likely), grad_block).reshape(window, D)
        d_probs = jnp.einsum("qhd,khd->hqk", grad_block, value_block)
        d_scores = rounded(likely * (d_probs - delta[:, :, None]))
        d_query = (jnp.einsum("hqk,khd->qhd", d_scores, key_block) * 0.125).reshape(TOK_DEV, D).astype(jnp.bfloat16)
        key_part = (jnp.einsum("hqk,qhd->khd", d_scores, query_block) * 0.125).reshape(window, D)
        key_acc = lax.dynamic_update_slice_in_dim(key_acc, lax.dynamic_slice_in_dim(key_acc, begin, window, 0) + rounded(key_part), begin, 0)
        value_acc = lax.dynamic_update_slice_in_dim(value_acc, lax.dynamic_slice_in_dim(value_acc, begin, window, 0) + rounded(value_part), begin, 0)
        return (key_acc, value_acc), (attn, d_query)

    zeros = jnp.zeros((TOKENS + 2 * margin, D), jnp.float32)
    (key_acc, value_acc), (attn_blocks, query_blocks) = lax.scan(block, (zeros, zeros), jnp.arange(N_CTX, dtype=jnp.int32))
    attn = attn_blocks.reshape(TOKENS, D)
    output = jnp.dot(attn, w_out, preferred_element_type=jnp.float32).astype(jnp.bfloat16)
    w_grad = jnp.dot(attn.T, d_out, preferred_element_type=jnp.float32)
    d_keys = key_acc[margin:margin + TOKENS].astype(jnp.bfloat16)
    d_values = value_acc[margin:margin + TOKENS].astype(jnp.bfloat16)
    return output, query_blocks.reshape(TOKENS, D), d_keys, d_values, w_grad


def reference(queries, keys, values, w_out, d_out, lengths):
    outputs, grads_q, grads_k, grads_v = [], [], [], []
    w_total = jnp.zeros((D, D), jnp.float32)
    for pack in range(PACKS):
        output, d_query, d_key, d_value, w_grad = one_pack(queries[pack], keys[pack], values[pack], w_out, d_out[pack], lengths[pack])
        outputs.append(output)
        grads_q.append(d_query)
        grads_k.append(d_key)
        grads_v.append(d_value)
        w_total = w_total + w_grad
    return jnp.stack(outputs), jnp.stack(grads_q), jnp.stack(grads_k), jnp.stack(grads_v), w_total
```

```python
import functools

import jax
import jax.numpy as jnp
from jax import lax
from jax.experimental import pallas as pl
from jax.experimental.pallas import tpu as pltpu
from jax.sharding import Mesh
from jax.sharding import PartitionSpec as P

HDIM = 64
HALVES = 2
MAXDOC = 1024
CHUNK = 256
VMEM_LIMIT = 48 * 1024 * 1024
SCALE = 0.125
EXP2_SCALE = SCALE * 1.4426950408889634
MASKED = -1e30

f32 = jnp.float32
bf16 = jnp.bfloat16


def params():
    return pltpu.CompilerParams(vmem_limit_bytes=VMEM_LIMIT)


def mm(a, b):
    return jnp.dot(a, b, preferred_element_type=f32)


def mm_nt(a, b):
    return lax.dot_general(a, b, (((1,), (1,)), ((), ())), preferred_element_type=f32)


def vmem():
    return pl.BlockSpec(memory_space=pltpu.VMEM)


def smem():
    return pl.BlockSpec(memory_space=pltpu.SMEM)


def prep_kernel(q_ref, k_ref, v_ref, g_ref, w_ref, len_ref, half_ref, qd_ref, kv_ref, st_ref, en_ref):
    heads = qd_ref.shape[0]
    own = st_ref.shape[0] * st_ref.shape[1]
    half = half_ref[0]
    grad = g_ref[...]
    for pair in range(heads // 2):
        cols = slice(pair * 128, pair * 128 + 128)
        k_t = k_ref[:, cols].T
        v_t = v_ref[:, cols].T
        q_t = q_ref[:, cols].T
        d_t = mm_nt(w_ref[cols, :], grad).astype(bf16)
        for side in range(2):
            rows = slice(side * HDIM, side * HDIM + HDIM)
            kv_ref[2 * pair + side, 0:HDIM, :] = k_t[rows]
            kv_ref[2 * pair + side, HDIM:, :] = v_t[rows]
            qd_ref[2 * pair + side, 0:HDIM, :] = q_t[rows]
            qd_ref[2 * pair + side, HDIM:, :] = d_t[rows]
    shape = st_ref.shape
    position = (
        lax.broadcasted_iota(jnp.int32, shape, 0) * shape[1]
        + lax.broadcasted_iota(jnp.int32, shape, 1)
        + half * own
    )

    def document(index, carry):
        end, begins, ends = carry
        end = end + len_ref[index]
        before = end <= position
        begins = jnp.where(before, end, begins)
        ends = jnp.where(before, ends, jnp.minimum(ends, end))
        return end, begins, ends

    _, begins, ends = lax.fori_loop(
        0,
        len_ref.shape[0],
        document,
        (jnp.int32(0), jnp.zeros(shape, jnp.int32), jnp.full(shape, 2 * own, jnp.int32)),
        unroll=8,
    )
    first = half * (own - MAXDOC)
    st_ref[...] = begins - first
    en_ref[...] = ends - first


def attention_kernel(
    half_ref, lo_ref, hi_ref, st_ref, en_ref, qd_ref, kv_ref, halo_ref,
    dqo_ref, dkv_ref, edge_ref, dhalo_ref,
    kv_t, kv_n, acc, probs,
):
    blocks, width, rows = qd_ref.shape
    edges = halo_ref.shape[0]
    half = half_ref[0]
    total = kv_t.shape[1]
    own_at = half * MAXDOC
    halo_at = (1 - half) * blocks * rows

    def place(index, source, start):
        at = pl.multiple_of(start + index * rows, rows)
        block = source[index]
        kv_t[:, pl.ds(at, rows)] = block
        kv_n[pl.ds(at, rows), :] = block.T
        acc[:, pl.ds(at, rows)] = jnp.zeros((width, rows), f32)

    @pl.loop(0, blocks)
    def _(index):
        place(index, kv_ref, own_at)

    @pl.loop(0, edges)
    def _(index):
        place(index, halo_ref, halo_at)

    feature = lax.broadcasted_iota(jnp.int32, (width, rows), 0)
    offset = lax.broadcasted_iota(jnp.int32, (CHUNK, rows), 0)

    @pl.loop(0, blocks)
    def _(index):
        qd = qd_ref[index]
        nothing = jnp.zeros_like(qd)
        query = jnp.where(feature < HDIM, qd, nothing)
        grad = jnp.where(feature < HDIM, nothing, qd)
        begin = st_ref[pl.ds(index, 1), :]
        end = en_ref[pl.ds(index, 1), :]
        low = (lo_ref[index] // 128) * 128
        count = (hi_ref[index] - low + CHUNK - 1) // CHUNK
        low = jnp.minimum(low, total - count * CHUNK)

        def at(chunk):
            return pl.multiple_of(low + chunk * CHUNK, 128)

        def slot(chunk):
            return pl.ds(pl.multiple_of(chunk * CHUNK, CHUNK), CHUNK)

        def score(chunk, top):
            base = at(chunk)
            scores = mm(kv_n[pl.ds(base, CHUNK), :], query)
            inside = (offset >= begin - base) & (offset < end - base)
            scores = jnp.where(inside, scores, MASKED)
            probs[slot(chunk), :] = scores
            return jnp.maximum(top, jnp.max(scores.reshape(CHUNK // 8, 8, rows), axis=0))

        top = lax.fori_loop(0, count, score, jnp.full((8, rows), MASKED, f32))
        top = jnp.max(top, axis=0, keepdims=True)

        def weigh(chunk, carry):
            sums, out = carry
            weights = jnp.exp2((probs[slot(chunk), :] - top) * EXP2_SCALE)
            probs[slot(chunk), :] = weights
            sums = sums + jnp.sum(weights.reshape(CHUNK // 8, 8, rows), axis=0)
            out = out + mm(kv_t[HDIM:, pl.ds(at(chunk), CHUNK)], weights.astype(bf16))
            return sums, out

        sums, out = lax.fori_loop(
            0, count, weigh, (jnp.zeros((8, rows), f32), jnp.zeros((HDIM, rows), f32))
        )
        inverse = 1.0 / jnp.sum(sums, axis=0, keepdims=True)
        attn = (out * inverse).astype(bf16)
        delta = jnp.sum(attn.astype(f32) * qd[HDIM:].astype(f32), axis=0, keepdims=True)

        def derive(chunk, d_query):
            base = at(chunk)
            likely = probs[slot(chunk), :] * inverse
            d_probs = mm(kv_n[pl.ds(base, CHUNK), :], grad)
            d_scores = (likely * (d_probs - delta)).astype(bf16)
            keys = pl.ds(base, CHUNK)
            acc[:HDIM, keys] += mm_nt(qd[:HDIM], d_scores)
            acc[HDIM:, keys] += mm_nt(qd[HDIM:], likely.astype(bf16))
            return d_query + mm(kv_t[:HDIM, keys], d_scores)

        d_query = lax.fori_loop(0, count, derive, jnp.zeros((HDIM, rows), f32))
        dqo_ref[index, :HDIM, :] = (d_query * SCALE).astype(bf16)
        dqo_ref[index, HDIM:, :] = attn

    factor = jnp.where(feature < HDIM, SCALE, 1.0)

    @pl.loop(0, blocks)
    def _(index):
        at = pl.multiple_of(own_at + index * rows, rows)
        dkv_ref[index] = (acc[:, pl.ds(at, rows)] * factor).astype(bf16)

    @pl.loop(0, edges)
    def _(index):
        at = pl.multiple_of(halo_at + index * rows, rows)
        dhalo_ref[index] = (acc[:, pl.ds(at, rows)] * factor).astype(bf16)
        at = pl.multiple_of(own_at + (1 - half) * (blocks - edges) * rows + index * rows, rows)
        edge_ref[index] = acc[:, pl.ds(at, rows)] * factor


def weight_kernel(dqo_ref, g_ref, w_grad_ref):
    heads = dqo_ref.shape[0]
    grad = g_ref[...]
    for four in range(heads // 4):
        attn_t = jnp.concatenate([dqo_ref[4 * four + n, HDIM:, :] for n in range(4)], axis=0)
        w_grad_ref[four * 256 : four * 256 + 256, :] = mm(attn_t, grad)


def output_kernel(dqo_ref, w_ref, out_ref, dq_ref):
    heads = dqo_ref.shape[0]
    parts = []
    for pair in range(heads // 2):
        cols = slice(pair * 128, pair * 128 + 128)
        both = [dqo_ref[2 * pair], dqo_ref[2 * pair + 1]]
        dq_ref[:, cols] = jnp.concatenate([b[:HDIM] for b in both], axis=0).T
        parts.append(jnp.concatenate([b[HDIM:] for b in both], axis=0).T)
    out_ref[...] = mm(jnp.concatenate(parts, axis=1), w_ref[...]).astype(bf16)


def split_kernel(dkv_ref, dk_ref, dv_ref):
    heads = dkv_ref.shape[0]
    for pair in range(heads // 2):
        cols = slice(pair * 128, pair * 128 + 128)
        both = [dkv_ref[2 * pair], dkv_ref[2 * pair + 1]]
        dk_ref[:, cols] = jnp.concatenate([b[:HDIM] for b in both], axis=0).T
        dv_ref[:, cols] = jnp.concatenate([b[HDIM:] for b in both], axis=0).T


def per_device(queries, keys, values, w_out, d_out, lengths):
    rows, width = queries.shape[1:]
    blocks = lax.axis_size("group")
    heads = width // HDIM
    edges = MAXDOC // rows
    half = lax.axis_index("half")
    half_scalar = half.reshape(1).astype(jnp.int32)
    pairs = jax.ShapeDtypeStruct((heads, 2 * HDIM, rows), bf16)
    bounds = jax.ShapeDtypeStruct((blocks, rows), jnp.int32)
    total = blocks * rows + MAXDOC
    most = MAXDOC * 2 + rows + CHUNK

    qd, kv, begins, ends = pl.pallas_call(
        prep_kernel,
        out_shape=(pairs, pairs, bounds, bounds),
        in_specs=[vmem()] * 5 + [smem()] * 2,
        out_specs=[vmem()] * 4,
        compiler_params=params(),
        name="prep",
    )(queries[0], keys[0], values[0], d_out[0], w_out, lengths[0], half_scalar)

    kv = lax.all_to_all(kv, "group", 0, 0, tiled=True)
    near = lax.dynamic_slice_in_dim(kv, (1 - half) * (blocks - edges), edges, 0)
    halo = lax.ppermute(near, "half", [(0, 1), (1, 0)])
    qd = lax.all_to_all(qd, "group", 0, 0, tiled=True)

    dqo, dkv, edge, dhalo = pl.pallas_call(
        attention_kernel,
        out_shape=(
            pairs,
            pairs,
            jax.ShapeDtypeStruct((edges, 2 * HDIM, rows), f32),
            jax.ShapeDtypeStruct((edges, 2 * HDIM, rows), bf16),
        ),
        in_specs=[smem()] * 3 + [vmem()] * 5,
        out_specs=[vmem()] * 4,
        scratch_shapes=[
            pltpu.VMEM((2 * HDIM, total), bf16),
            pltpu.VMEM((total, 2 * HDIM), bf16),
            pltpu.VMEM((2 * HDIM, total), f32),
            pltpu.VMEM((most, rows), f32),
        ],
        compiler_params=params(),
        name="attention",
    )(half_scalar, begins[:, 0], ends[:, rows - 1], begins, ends, qd, kv, halo)

    dhalo = lax.ppermute(dhalo, "half", [(0, 1), (1, 0)])
    dqo = lax.all_to_all(dqo, "group", 0, 0, tiled=True)
    w_grad = pl.pallas_call(
        weight_kernel,
        out_shape=jax.ShapeDtypeStruct((width, width), f32),
        in_specs=[vmem()] * 2,
        out_specs=vmem(),
        compiler_params=params(),
        name="weight",
    )(dqo, d_out[0])
    w_grad = lax.psum_scatter(w_grad, ("half", "group"), scatter_dimension=0, tiled=True)

    edge = (edge + dhalo.astype(f32)).astype(bf16)
    dkv = lax.dynamic_update_slice_in_dim(dkv, edge, (1 - half) * (blocks - edges), 0)
    dkv = lax.all_to_all(dkv, "group", 0, 0, tiled=True)
    flat = jax.ShapeDtypeStruct((rows, width), bf16)
    output, d_queries = pl.pallas_call(
        output_kernel,
        out_shape=(flat, flat),
        in_specs=[vmem()] * 2,
        out_specs=[vmem()] * 2,
        compiler_params=params(),
        name="output",
    )(dqo, w_out)
    d_keys, d_values = pl.pallas_call(
        split_kernel,
        out_shape=(flat, flat),
        in_specs=[vmem()],
        out_specs=[vmem()] * 2,
        compiler_params=params(),
        name="split",
    )(dkv)
    dp_count = lax.axis_size("dp")
    w_grad = lax.all_to_all(w_grad.reshape(dp_count, -1, width), "dp", 0, 0, tiled=True)
    w_grad = jnp.sum(w_grad, axis=0)
    return (output[None], d_queries[None], d_keys[None], d_values[None], w_grad)


def solution(mesh):
    ctx_count, dp_count = mesh.devices.shape
    fine = Mesh(
        mesh.devices.reshape(HALVES, ctx_count // HALVES, dp_count), ("half", "group", "dp")
    )
    tokens = P("dp", ("half", "group"), None)
    return jax.shard_map(
        per_device,
        mesh=fine,
        in_specs=(tokens, tokens, tokens, P(), tokens, P("dp", None)),
        out_specs=(tokens, tokens, tokens, tokens, P(("half", "group", "dp"), None)),
        check_vma=False,
    )
```

```python
import jax
import jax.numpy as jnp
from jax import lax
from jax.experimental import pallas as pl
from jax.experimental.pallas import tpu as pltpu
from jax.sharding import Mesh
from jax.sharding import PartitionSpec as P

HDIM = 64
HALVES = 2
CORES = 2
MAXDOC = 1024
CHUNK = 256
STATIC_COUNTS = (2, 3, 4, 5, 6)
VMEM_LIMIT = 48 * 1024 * 1024
SCALE = 0.125
LOG2E = 1.4426950408889634
EXP2_SCALE = SCALE * LOG2E
MASKED = -1e30

f32 = jnp.float32
bf16 = jnp.bfloat16


def mm(a, b):
    return jnp.dot(a, b, preferred_element_type=f32)


def mm_nt(a, b):
    return lax.dot_general(a, b, (((1,), (1,)), ((), ())), preferred_element_type=f32)


def vmem(count):
    return [pl.BlockSpec(memory_space=pltpu.VMEM)] * count


def smem(count):
    return [pl.BlockSpec(memory_space=pltpu.SMEM)] * count


def call(kernel, name, out_shape, in_specs, scratch=(), flops=0, touched=0, *, args):
    many = isinstance(out_shape, tuple)
    return pl.pallas_call(
        kernel,
        out_shape=out_shape,
        in_specs=in_specs,
        out_specs=vmem(len(out_shape)) if many else vmem(1)[0],
        scratch_shapes=list(scratch),
        compiler_params=pltpu.CompilerParams(vmem_limit_bytes=VMEM_LIMIT),
        cost_estimate=pl.CostEstimate(flops=flops, bytes_accessed=touched, transcendentals=0),
        name=name,
    )(*args)


def prep_kernel(q_ref, k_ref, v_ref, len_ref, half_ref, qkv_ref, st_ref, en_ref):
    heads = qkv_ref.shape[0]
    own = st_ref.shape[0] * st_ref.shape[1]
    half = half_ref[0]
    for pair in range(heads // 2):
        cols = slice(pair * 128, pair * 128 + 128)
        for place, source in enumerate((q_ref, k_ref, v_ref)):
            turned = source[:, cols].T
            for side in range(2):
                qkv_ref[2 * pair + side, place * HDIM : place * HDIM + HDIM, :] = turned[
                    side * HDIM : side * HDIM + HDIM
                ]
    shape = st_ref.shape
    position = (
        lax.broadcasted_iota(jnp.int32, shape, 0) * shape[1]
        + lax.broadcasted_iota(jnp.int32, shape, 1)
        + half * own
    )

    def document(index, carry):
        end, begins, ends = carry
        end = end + len_ref[index]
        before = end <= position
        begins = jnp.where(before, end, begins)
        ends = jnp.where(before, ends, jnp.minimum(ends, end))
        return end, begins, ends

    _, begins, ends = lax.fori_loop(
        0,
        len_ref.shape[0],
        document,
        (jnp.int32(0), jnp.zeros(shape, jnp.int32), jnp.full(shape, 2 * own, jnp.int32)),
        unroll=8,
    )
    first = half * (own - MAXDOC)
    st_ref[...] = begins - first
    en_ref[...] = ends - first


def project_kernel(g_ref, w_ref, da_ref):
    grad = g_ref[...]
    for four in range(da_ref.shape[0] // 4):
        part = mm_nt(w_ref[four * 256 : four * 256 + 256, :], grad).astype(bf16)
        for n in range(4):
            da_ref[4 * four + n] = part[n * HDIM : n * HDIM + HDIM]


def span(lo_ref, hi_ref, index):
    low = (lo_ref[index] // 128) * 128
    return low, (hi_ref[index] - low + CHUNK - 1) // CHUNK


def by_count(low, count, total, run):
    for fixed in STATIC_COUNTS:
        here = count == fixed if fixed > STATIC_COUNTS[0] else count <= fixed

        @pl.when(here)
        def _(fixed=fixed):
            run(jnp.minimum(low, total - fixed * CHUNK), fixed)

    @pl.when(count > STATIC_COUNTS[-1])
    def _():
        run(jnp.minimum(low, total - count * CHUNK), count)


def over(count, body, carry):
    if isinstance(count, int):
        for chunk in range(count):
            carry = body(chunk, carry)
        return carry
    return lax.fori_loop(0, count, body, carry)


def chunk_rows(chunk):
    start = chunk * CHUNK
    return pl.ds(start if isinstance(chunk, int) else pl.multiple_of(start, CHUNK), CHUNK)


def forward_kernel(
    half_ref, lo_ref, hi_ref, st_ref, en_ref, qkv_ref, halo_ref,
    attn_ref, stat_ref, kv_n, k_t, v_t, probs,
):
    blocks, _, rows = qkv_ref.shape
    edges = halo_ref.shape[0]
    half = half_ref[0]
    total = kv_n.shape[0]

    def place(block, at):
        at = pl.multiple_of(at, rows)
        k_t[:, pl.ds(at, rows)] = block[:HDIM]
        v_t[:, pl.ds(at, rows)] = block[HDIM:]
        kv_n[pl.ds(at, rows), :] = block.T

    @pl.loop(0, blocks)
    def _(index):
        place(qkv_ref[index, HDIM:, :], half * MAXDOC + index * rows)

    @pl.loop(0, edges)
    def _(index):
        place(halo_ref[index], (1 - half) * blocks * rows + index * rows)

    offset = lax.broadcasted_iota(jnp.int32, (CHUNK, rows), 0)

    @pl.loop(0, blocks)
    def _(index):
        query = qkv_ref[index, :HDIM, :]
        query = jnp.concatenate([query, jnp.zeros_like(query)], axis=0)
        begin = st_ref[pl.ds(index, 1), :]
        end = en_ref[pl.ds(index, 1), :]

        def run(low, count):
            def at(chunk):
                return pl.multiple_of(low + chunk * CHUNK, 128)

            def score(chunk, top):
                base = at(chunk)
                scores = mm(kv_n[pl.ds(base, CHUNK), :], query)
                inside = (offset >= begin - base) & (offset < end - base)
                scores = jnp.where(inside, scores, MASKED)
                probs[chunk_rows(chunk), :] = scores
                return jnp.maximum(top, jnp.max(scores.reshape(CHUNK // 8, 8, rows), axis=0))

            top = over(count, score, jnp.full((8, rows), MASKED, f32))
            top = jnp.max(top, axis=0, keepdims=True)

            def weigh(chunk, carry):
                sums, out = carry
                weights = jnp.exp2((probs[chunk_rows(chunk), :] - top) * EXP2_SCALE)
                sums = sums + jnp.sum(weights.reshape(CHUNK // 8, 8, rows), axis=0)
                out = out + mm(v_t[:, pl.ds(at(chunk), CHUNK)], weights.astype(bf16))
                return sums, out

            sums, out = over(
                count, weigh, (jnp.zeros((8, rows), f32), jnp.zeros((HDIM, rows), f32))
            )
            sums = jnp.sum(sums, axis=0, keepdims=True)
            attn_ref[index] = (out * (1.0 / sums)).astype(bf16)
            stat_ref[pl.ds(index, 1), :] = top * EXP2_SCALE + jnp.log(sums) * LOG2E

        low, count = span(lo_ref, hi_ref, index)
        by_count(low, count, total, run)


def backward_kernel(
    half_ref, lo_ref, hi_ref, st_ref, en_ref, qkv_ref, da_ref, attn_ref, stat_ref, kv_n, k_t,
    grads_ref, edge_ref, dhalo_ref, acc,
):
    blocks, _, rows = qkv_ref.shape
    edges = edge_ref.shape[0]
    half = half_ref[0]
    total = kv_n.shape[0]

    @pl.loop(0, total // CHUNK)
    def _(chunk):
        acc[:, chunk_rows(chunk)] = jnp.zeros((acc.shape[0], CHUNK), f32)

    offset = lax.broadcasted_iota(jnp.int32, (CHUNK, rows), 0)

    @pl.loop(0, blocks)
    def _(index):
        query_t = qkv_ref[index, :HDIM, :]
        grad_t = da_ref[index]
        nothing = jnp.zeros_like(query_t)
        query = jnp.concatenate([query_t, nothing], axis=0)
        grad = jnp.concatenate([nothing, grad_t], axis=0)
        begin = st_ref[pl.ds(index, 1), :]
        end = en_ref[pl.ds(index, 1), :]
        log_total = stat_ref[pl.ds(index, 1), :]
        delta = jnp.sum(
            attn_ref[index].astype(f32) * grad_t.astype(f32), axis=0, keepdims=True
        )

        def run(low, count):
            def derive(chunk, d_query):
                base = pl.multiple_of(low + chunk * CHUNK, 128)
                keys = pl.ds(base, CHUNK)
                both = kv_n[keys, :]
                scores = mm(both, query)
                d_probs = mm(both, grad)
                inside = (offset >= begin - base) & (offset < end - base)
                likely = jnp.where(inside, jnp.exp2(scores * EXP2_SCALE - log_total), 0.0)
                d_scores = (likely * (d_probs - delta)).astype(bf16)
                acc[:HDIM, keys] += mm_nt(query_t, d_scores)
                acc[HDIM:, keys] += mm_nt(grad_t, likely.astype(bf16))
                return d_query + mm(k_t[:, keys], d_scores)

            d_query = over(count, derive, jnp.zeros((HDIM, rows), f32))
            grads_ref[index, :HDIM, :] = (d_query * SCALE).astype(bf16)

        low, count = span(lo_ref, hi_ref, index)
        by_count(low, count, total, run)

    feature = lax.broadcasted_iota(jnp.int32, (2 * HDIM, rows), 0)
    factor = jnp.where(feature < HDIM, SCALE, 1.0)
    own_at = half * MAXDOC

    @pl.loop(0, blocks)
    def _(index):
        at = pl.multiple_of(own_at + index * rows, rows)
        grads_ref[index, HDIM:, :] = (acc[:, pl.ds(at, rows)] * factor).astype(bf16)

    @pl.loop(0, edges)
    def _(index):
        at = pl.multiple_of((1 - half) * blocks * rows + index * rows, rows)
        dhalo_ref[index] = (acc[:, pl.ds(at, rows)] * factor).astype(bf16)
        at = pl.multiple_of(own_at + (1 - half) * (blocks - edges) * rows + index * rows, rows)
        edge_ref[index] = acc[:, pl.ds(at, rows)] * factor


def weight_kernel(core_ref, attn_ref, g_ref, keep_ref, send_ref):
    grad = g_ref[...]
    mine = core_ref[0] == 0
    side = HDIM // CORES
    for four in range(attn_ref.shape[0] // 4):
        attn_t = jnp.concatenate([attn_ref[4 * four + n] for n in range(4)], axis=0)
        part = mm(attn_t, grad)
        for n in range(4):
            lower = part[n * HDIM : n * HDIM + side]
            upper = part[n * HDIM + side : n * HDIM + HDIM]
            keep_ref[4 * four + n] = jnp.where(mine, lower, upper)
            send_ref[4 * four + n] = jnp.where(mine, upper, lower).astype(bf16)


def output_kernel(attn_ref, w_ref, out_ref):
    parts = [
        jnp.concatenate([attn_ref[2 * pair], attn_ref[2 * pair + 1]], axis=0).T
        for pair in range(attn_ref.shape[0] // 2)
    ]
    out_ref[...] = mm(jnp.concatenate(parts, axis=1), w_ref[...]).astype(bf16)


def split_kernel(grads_ref, dq_ref, dk_ref, dv_ref):
    for pair in range(grads_ref.shape[0] // 2):
        cols = slice(pair * 128, pair * 128 + 128)
        for place, target in enumerate((dq_ref, dk_ref, dv_ref)):
            rows = slice(place * HDIM, place * HDIM + HDIM)
            both = [grads_ref[2 * pair + side, rows, :] for side in range(2)]
            target[:, cols] = jnp.concatenate(both, axis=0).T


def per_device(queries, keys, values, w_out, d_out, lengths):
    rows, width = queries.shape[1:]
    group = ("pair", "core")
    blocks = lax.axis_size(group)
    heads = width // HDIM
    edges = MAXDOC // rows
    half = lax.axis_index("half")
    half_scalar = half.reshape(1).astype(jnp.int32)
    core_scalar = lax.axis_index("core").reshape(1).astype(jnp.int32)
    total = blocks * rows + MAXDOC
    most = MAXDOC * 2 + rows + CHUNK
    shape = jax.ShapeDtypeStruct
    swap = [(0, 1), (1, 0)]

    qkv, begins, ends = call(
        prep_kernel,
        "prep",
        (shape((heads, 3 * HDIM, rows), bf16),) + (shape((blocks, rows), jnp.int32),) * 2,
        vmem(3) + smem(2),
        args=(queries[0], keys[0], values[0], lengths[0], half_scalar),
    )
    lows, highs = begins[:, 0], ends[:, rows - 1]
    d_attn = call(
        project_kernel,
        "project",
        shape((heads, HDIM, rows), bf16),
        vmem(2),
        flops=2 * rows * width * width,
        touched=2 * width * width,
        args=(d_out[0], w_out),
    )
    qkv = lax.all_to_all(qkv, group, 0, 0, tiled=True)
    near = lax.dynamic_slice_in_dim(qkv, (1 - half) * (blocks - edges), edges, 0)[:, HDIM:]
    halo = lax.ppermute(near, "half", swap)
    d_attn = lax.all_to_all(d_attn, group, 0, 0, tiled=True)

    attn, stats, kv_n, k_t = call(
        forward_kernel,
        "forward",
        (
            shape((blocks, HDIM, rows), bf16),
            shape((blocks, rows), f32),
            shape((total, 2 * HDIM), bf16),
            shape((HDIM, total), bf16),
        ),
        smem(3) + vmem(4),
        (pltpu.VMEM((HDIM, total), bf16), pltpu.VMEM((most, rows), f32)),
        flops=10**10,
        touched=10**7,
        args=(half_scalar, lows, highs, begins, ends, qkv, halo),
    )
    grads, edge, dhalo = call(
        backward_kernel,
        "backward",
        (
            shape((blocks, 3 * HDIM, rows), bf16),
            shape((edges, 2 * HDIM, rows), f32),
            shape((edges, 2 * HDIM, rows), bf16),
        ),
        smem(3) + vmem(8),
        (pltpu.VMEM((2 * HDIM, total), f32),),
        flops=10**10,
        touched=10**7,
        args=(half_scalar, lows, highs, begins, ends, qkv, d_attn, attn, stats, kv_n, k_t),
    )
    attn = lax.all_to_all(attn, group, 0, 0, tiled=True)
    dhalo = lax.ppermute(dhalo, "half", swap)
    edge = (edge + dhalo.astype(f32)).astype(bf16)
    grads = lax.dynamic_update_slice(grads, edge, ((1 - half) * (blocks - edges), HDIM, 0))
    grads = lax.all_to_all(grads, group, 0, 0, tiled=True)

    side = HDIM // CORES
    keep, send = call(
        weight_kernel,
        "weight",
        (shape((heads, side, width), f32), shape((heads, side, width), bf16)),
        smem(1) + vmem(2),
        flops=2 * rows * width * width,
        touched=6 * width * width,
        args=(core_scalar, attn, d_out[0]),
    )
    other = lax.ppermute(send, "core", swap)
    chip_sum = (keep + other.astype(f32)).astype(bf16).reshape(-1, 8, width)
    parts = lax.all_to_all(chip_sum, ("half", "pair", "dp"), 0, 0, tiled=True)
    w_grad = jnp.sum(parts.astype(f32), axis=0)

    flat = shape((rows, width), bf16)
    output = call(
        output_kernel,
        "output",
        flat,
        vmem(2),
        flops=2 * rows * width * width,
        touched=2 * width * width,
        args=(attn, w_out),
    )
    d_queries, d_keys, d_values = call(
        split_kernel, "split", (flat,) * 3, vmem(1), args=(grads,)
    )
    return (output[None], d_queries[None], d_keys[None], d_values[None], w_grad)


def solution(mesh):
    ctx_count, dp_count = mesh.devices.shape
    pairs = ctx_count // (HALVES * CORES)
    fine = Mesh(
        mesh.devices.reshape(HALVES, pairs, CORES, dp_count), ("half", "pair", "core", "dp")
    )
    ctx = ("half", "pair", "core")
    tokens = P("dp", ctx, None)
    return jax.shard_map(
        per_device,
        mesh=fine,
        in_specs=(tokens, tokens, tokens, P(), tokens, P("dp", None)),
        out_specs=(tokens, tokens, tokens, tokens, P(ctx + ("dp",), None)),
        check_vma=False,
    )
```

```python
import jax
import jax.numpy as jnp
from jax import lax
from jax.experimental import pallas as pl
from jax.experimental.pallas import tpu as pltpu
from jax.sharding import Mesh
from jax.sharding import PartitionSpec as P

HDIM = 64
HALVES = 2
CORES = 2
MAXDOC = 1024
CHUNK = 256
STATIC_COUNTS = (2, 3, 4, 5, 6)
VMEM_LIMIT = 60 * 1024 * 1024
SCALE = 0.125
LOG2E = 1.4426950408889634
EXP2_SCALE = SCALE * LOG2E
MASKED = -1e30

f32 = jnp.float32
bf16 = jnp.bfloat16


def mm(a, b):
    return jnp.dot(a, b, preferred_element_type=f32)


def mm_nt(a, b):
    return lax.dot_general(a, b, (((1,), (1,)), ((), ())), preferred_element_type=f32)


def vmem(count):
    return [pl.BlockSpec(memory_space=pltpu.VMEM)] * count


def smem(count):
    return [pl.BlockSpec(memory_space=pltpu.SMEM)] * count


def call(kernel, name, out_shape, in_specs, scratch=(), flops=0, touched=0, *, args):
    many = isinstance(out_shape, tuple)
    return pl.pallas_call(
        kernel,
        out_shape=out_shape,
        in_specs=in_specs,
        out_specs=vmem(len(out_shape)) if many else vmem(1)[0],
        scratch_shapes=list(scratch),
        compiler_params=pltpu.CompilerParams(vmem_limit_bytes=VMEM_LIMIT),
        cost_estimate=pl.CostEstimate(flops=flops, bytes_accessed=touched, transcendentals=0),
        name=name,
    )(*args)


def prep_kernel(q_ref, k_ref, v_ref, len_ref, half_ref, qkv_ref, st_ref, en_ref):
    heads = qkv_ref.shape[0]
    own = st_ref.shape[0] * st_ref.shape[1]
    half = half_ref[0]
    for pair in range(heads // 2):
        cols = slice(pair * 128, pair * 128 + 128)
        for place, source in enumerate((q_ref, k_ref, v_ref)):
            turned = source[:, cols].T
            for side in range(2):
                qkv_ref[2 * pair + side, place * HDIM : place * HDIM + HDIM, :] = turned[
                    side * HDIM : side * HDIM + HDIM
                ]
    shape = st_ref.shape
    position = (
        lax.broadcasted_iota(jnp.int32, shape, 0) * shape[1]
        + lax.broadcasted_iota(jnp.int32, shape, 1)
        + half * own
    )

    def document(index, carry):
        end, begins, ends = carry
        end = end + len_ref[index]
        before = end <= position
        begins = jnp.where(before, end, begins)
        ends = jnp.where(before, ends, jnp.minimum(ends, end))
        return end, begins, ends

    _, begins, ends = lax.fori_loop(
        0,
        len_ref.shape[0],
        document,
        (jnp.int32(0), jnp.zeros(shape, jnp.int32), jnp.full(shape, 2 * own, jnp.int32)),
        unroll=8,
    )
    first = half * (own - MAXDOC)
    st_ref[...] = begins - first
    en_ref[...] = ends - first


def project_kernel(g_ref, w_ref, da_ref):
    grad = g_ref[...]
    for four in range(da_ref.shape[0] // 4):
        part = mm_nt(w_ref[four * 256 : four * 256 + 256, :], grad).astype(bf16)
        for n in range(4):
            da_ref[4 * four + n] = part[n * HDIM : n * HDIM + HDIM]


def span(lo_ref, hi_ref, index):
    low = (lo_ref[index] // 128) * 128
    return low, (hi_ref[index] - low + CHUNK - 1) // CHUNK


def by_count(low, count, total, run):
    for fixed in STATIC_COUNTS:
        here = count == fixed if fixed > STATIC_COUNTS[0] else count <= fixed

        @pl.when(here)
        def _(fixed=fixed):
            run(jnp.minimum(low, total - fixed * CHUNK), fixed)

    @pl.when(count > STATIC_COUNTS[-1])
    def _():
        run(jnp.minimum(low, total - count * CHUNK), count)


def over(count, body, carry):
    if isinstance(count, int):
        for chunk in range(count):
            carry = body(chunk, carry)
        return carry
    return lax.fori_loop(0, count, body, carry)


def chunk_rows(chunk):
    start = chunk * CHUNK
    return pl.ds(start if isinstance(chunk, int) else pl.multiple_of(start, CHUNK), CHUNK)


def forward_kernel(
    half_ref, lo_ref, hi_ref, st_ref, en_ref, qkv_ref, halo_ref,
    attn_ref, stat_ref, kv_n, k_t, v_t, probs,
):
    blocks, _, rows = qkv_ref.shape
    edges = halo_ref.shape[0]
    half = half_ref[0]
    total = kv_n.shape[0]

    def place(block, at):
        at = pl.multiple_of(at, rows)
        k_t[:, pl.ds(at, rows)] = block[:HDIM]
        v_t[:, pl.ds(at, rows)] = block[HDIM:]
        kv_n[pl.ds(at, rows), :] = block.T

    @pl.loop(0, blocks)
    def _(index):
        place(qkv_ref[index, HDIM:, :], half * MAXDOC + index * rows)

    @pl.loop(0, edges)
    def _(index):
        place(halo_ref[index], (1 - half) * blocks * rows + index * rows)

    offset = lax.broadcasted_iota(jnp.int32, (CHUNK, rows), 0)

    @pl.loop(0, blocks)
    def _(index):
        query = qkv_ref[index, :HDIM, :]
        query = jnp.concatenate([query, jnp.zeros_like(query)], axis=0)
        begin = st_ref[pl.ds(index, 1), :]
        end = en_ref[pl.ds(index, 1), :]

        def run(low, count):
            def at(chunk):
                return pl.multiple_of(low + chunk * CHUNK, 128)

            def score(chunk, top):
                base = at(chunk)
                scores = mm(kv_n[pl.ds(base, CHUNK), :], query)
                inside = (offset >= begin - base) & (offset < end - base)
                scores = jnp.where(inside, scores, MASKED)
                probs[chunk_rows(chunk), :] = scores
                return jnp.maximum(top, jnp.max(scores.reshape(CHUNK // 8, 8, rows), axis=0))

            top = over(count, score, jnp.full((8, rows), MASKED, f32))
            top = jnp.max(top, axis=0, keepdims=True)

            def weigh(chunk, carry):
                sums, out = carry
                weights = jnp.exp2((probs[chunk_rows(chunk), :] - top) * EXP2_SCALE)
                sums = sums + jnp.sum(weights.reshape(CHUNK // 8, 8, rows), axis=0)
                out = out + mm(v_t[:, pl.ds(at(chunk), CHUNK)], weights.astype(bf16))
                return sums, out

            sums, out = over(
                count, weigh, (jnp.zeros((8, rows), f32), jnp.zeros((HDIM, rows), f32))
            )
            sums = jnp.sum(sums, axis=0, keepdims=True)
            attn = (out * (1.0 / sums)).astype(bf16)
            attn_ref[index, :HDIM, :] = attn
            side = HDIM // CORES
            sibling = index + 1 - 2 * (index % CORES)
            attn_ref[sibling, HDIM:, :] = jnp.where(
                index % CORES == 0, attn[side:], attn[:side]
            )
            stat_ref[pl.ds(index, 1), :] = top * EXP2_SCALE + jnp.log(sums) * LOG2E

        low, count = span(lo_ref, hi_ref, index)
        by_count(low, count, total, run)


def backward_kernel(
    half_ref, lo_ref, hi_ref, st_ref, en_ref, qkv_ref, da_ref, attn_ref, stat_ref, kv_n, k_t,
    grads_ref, edge_ref, dhalo_ref, acc,
):
    blocks, _, rows = qkv_ref.shape
    edges = edge_ref.shape[0]
    half = half_ref[0]
    total = kv_n.shape[0]

    @pl.loop(0, total // CHUNK)
    def _(chunk):
        acc[:, chunk_rows(chunk)] = jnp.zeros((acc.shape[0], CHUNK), f32)

    offset = lax.broadcasted_iota(jnp.int32, (CHUNK, rows), 0)

    @pl.loop(0, blocks)
    def _(index):
        query_t = qkv_ref[index, :HDIM, :]
        grad_t = da_ref[index]
        nothing = jnp.zeros_like(query_t)
        query = jnp.concatenate([query_t, nothing], axis=0)
        grad = jnp.concatenate([nothing, grad_t], axis=0)
        begin = st_ref[pl.ds(index, 1), :]
        end = en_ref[pl.ds(index, 1), :]
        log_total = stat_ref[pl.ds(index, 1), :]
        delta = jnp.sum(
            attn_ref[index, :HDIM, :].astype(f32) * grad_t.astype(f32), axis=0, keepdims=True
        )

        def run(low, count):
            def derive(chunk, d_query):
                base = pl.multiple_of(low + chunk * CHUNK, 128)
                keys = pl.ds(base, CHUNK)
                both = kv_n[keys, :]
                scores = mm(both, query)
                d_probs = mm(both, grad)
                inside = (offset >= begin - base) & (offset < end - base)
                likely = jnp.where(inside, jnp.exp2(scores * EXP2_SCALE - log_total), 0.0)
                d_scores = (likely * (d_probs - delta)).astype(bf16)
                acc[:HDIM, keys] += mm_nt(query_t, d_scores)
                acc[HDIM:, keys] += mm_nt(grad_t, likely.astype(bf16))
                return d_query + mm(k_t[:, keys], d_scores)

            d_query = over(count, derive, jnp.zeros((HDIM, rows), f32))
            grads_ref[index, :HDIM, :] = (d_query * SCALE).astype(bf16)

        low, count = span(lo_ref, hi_ref, index)
        by_count(low, count, total, run)

    feature = lax.broadcasted_iota(jnp.int32, (2 * HDIM, rows), 0)
    factor = jnp.where(feature < HDIM, SCALE, 1.0)
    own_at = half * MAXDOC

    @pl.loop(0, blocks)
    def _(index):
        at = pl.multiple_of(own_at + index * rows, rows)
        grads_ref[index, HDIM:, :] = (acc[:, pl.ds(at, rows)] * factor).astype(bf16)

    @pl.loop(0, edges)
    def _(index):
        at = pl.multiple_of((1 - half) * blocks * rows + index * rows, rows)
        dhalo_ref[index] = (acc[:, pl.ds(at, rows)] * factor).astype(bf16)
        at = pl.multiple_of(own_at + (1 - half) * (blocks - edges) * rows + index * rows, rows)
        edge_ref[index] = acc[:, pl.ds(at, rows)] * factor


def weight_kernel(core_ref, attn_ref, g_ref, sibling_ref, out_ref):
    grad, sibling_grad = g_ref[...], sibling_ref[...]
    mine = core_ref[0] == 0
    side = HDIM // CORES
    dp_count, heads = out_ref.shape[:2]
    size = side // dp_count
    own, sibling = [], []
    for head in range(heads):
        rows = attn_ref[head, :HDIM, :]
        own.append(jnp.where(mine, rows[:side], rows[side:]))
        sibling.append(attn_ref[head, HDIM:, :])
    for part in range(2):
        some = slice(part * heads // 2, (part + 1) * heads // 2)
        total = mm(jnp.concatenate(own[some], axis=0), grad)
        total += mm(jnp.concatenate(sibling[some], axis=0), sibling_grad)
        for n, head in enumerate(range(heads)[some]):
            for place in range(dp_count):
                at = n * side + place * size
                out_ref[place, head] = total[at : at + size].astype(bf16)


def output_kernel(attn_ref, w_ref, out_ref):
    parts = [
        jnp.concatenate(
            [attn_ref[2 * pair + side, :HDIM, :] for side in range(2)], axis=0
        ).T
        for pair in range(attn_ref.shape[0] // 2)
    ]
    out_ref[...] = mm(jnp.concatenate(parts, axis=1), w_ref[...]).astype(bf16)


def split_kernel(grads_ref, dq_ref, dk_ref, dv_ref):
    for pair in range(grads_ref.shape[0] // 2):
        cols = slice(pair * 128, pair * 128 + 128)
        for place, target in enumerate((dq_ref, dk_ref, dv_ref)):
            rows = slice(place * HDIM, place * HDIM + HDIM)
            both = [grads_ref[2 * pair + side, rows, :] for side in range(2)]
            target[:, cols] = jnp.concatenate(both, axis=0).T


def per_device(queries, keys, values, w_out, d_out, lengths):
    rows, width = queries.shape[1:]
    group = ("pair", "core")
    blocks = lax.axis_size(group)
    heads = width // HDIM
    edges = MAXDOC // rows
    half = lax.axis_index("half")
    half_scalar = half.reshape(1).astype(jnp.int32)
    side = HDIM // CORES
    dp_count = lax.axis_size("dp")
    core_scalar = lax.axis_index("core").reshape(1).astype(jnp.int32)
    total = blocks * rows + MAXDOC
    most = MAXDOC * 2 + rows + CHUNK
    shape = jax.ShapeDtypeStruct
    swap = [(0, 1), (1, 0)]

    qkv, begins, ends = call(
        prep_kernel,
        "prep",
        (shape((heads, 3 * HDIM, rows), bf16),) + (shape((blocks, rows), jnp.int32),) * 2,
        vmem(3) + smem(2),
        args=(queries[0], keys[0], values[0], lengths[0], half_scalar),
    )
    lows, highs = begins[:, 0], ends[:, rows - 1]
    d_attn = call(
        project_kernel,
        "project",
        shape((heads, HDIM, rows), bf16),
        vmem(2),
        flops=2 * rows * width * width,
        touched=2 * width * width,
        args=(d_out[0], w_out),
    )
    sibling_grad = lax.ppermute(d_out[0], "core", swap)
    qkv = lax.all_to_all(qkv, group, 0, 0, tiled=True)
    qkv, d_attn = lax.optimization_barrier((qkv, d_attn))
    near = lax.dynamic_slice_in_dim(qkv, (1 - half) * (blocks - edges), edges, 0)[:, HDIM:]
    halo = lax.ppermute(near, "half", swap)
    d_attn = lax.all_to_all(d_attn, group, 0, 0, tiled=True)

    attn, stats, kv_n, k_t = call(
        forward_kernel,
        "forward",
        (
            shape((blocks, HDIM + side, rows), bf16),
            shape((blocks, rows), f32),
            shape((total, 2 * HDIM), bf16),
            shape((HDIM, total), bf16),
        ),
        smem(3) + vmem(4),
        (pltpu.VMEM((HDIM, total), bf16), pltpu.VMEM((most, rows), f32)),
        flops=10**10,
        touched=10**7,
        args=(half_scalar, lows, highs, begins, ends, qkv, halo),
    )
    grads, edge, dhalo = call(
        backward_kernel,
        "backward",
        (
            shape((blocks, 3 * HDIM, rows), bf16),
            shape((edges, 2 * HDIM, rows), f32),
            shape((edges, 2 * HDIM, rows), bf16),
        ),
        smem(3) + vmem(8),
        (pltpu.VMEM((2 * HDIM, total), f32),),
        flops=10**10,
        touched=10**7,
        args=(half_scalar, lows, highs, begins, ends, qkv, d_attn, attn, stats, kv_n, k_t),
    )
    attn = lax.all_to_all(attn, group, 0, 0, tiled=True)
    dhalo = lax.ppermute(dhalo, "half", swap)
    attn, grads, edge = lax.optimization_barrier((attn, grads, edge))
    chip_sum = call(
        weight_kernel,
        "weight",
        shape((dp_count, heads, side // dp_count, width), bf16),
        smem(1) + vmem(3),
        flops=2 * rows * width * width,
        touched=4 * width * width,
        args=(core_scalar, attn, d_out[0], sibling_grad),
    )
    dhalo, chip_sum = lax.optimization_barrier((dhalo, chip_sum))
    mine = lax.axis_index("dp")
    column = lax.dynamic_index_in_dim(chip_sum, mine, 0, keepdims=False).astype(f32)
    for step in range(1, dp_count):
        part = lax.dynamic_index_in_dim(chip_sum, (mine + step) % dp_count, 0, keepdims=False)
        moves = [(d, (d + step) % dp_count) for d in range(dp_count)]
        column = column + lax.ppermute(part, "dp", moves).astype(f32)

    edge = (edge + dhalo.astype(f32)).astype(bf16)
    grads = lax.dynamic_update_slice(grads, edge, ((1 - half) * (blocks - edges), HDIM, 0))
    grads = lax.all_to_all(grads, group, 0, 0, tiled=True)
    column, grads = lax.optimization_barrier((column.astype(bf16), grads))
    parts = lax.all_to_all(column, ("half", "pair"), 0, 0, tiled=True)
    w_grad = jnp.sum(parts.astype(f32), axis=0)

    flat = shape((rows, width), bf16)
    output = call(
        output_kernel,
        "output",
        flat,
        vmem(2),
        flops=2 * rows * width * width,
        touched=2 * width * width,
        args=(attn, w_out),
    )
    d_queries, d_keys, d_values = call(
        split_kernel, "split", (flat,) * 3, vmem(1), args=(grads,)
    )
    return (output[None], d_queries[None], d_keys[None], d_values[None], w_grad)


def solution(mesh):
    ctx_count, dp_count = mesh.devices.shape
    pairs = ctx_count // (HALVES * CORES)
    fine = Mesh(
        mesh.devices.reshape(HALVES, pairs, CORES, dp_count), ("half", "pair", "core", "dp")
    )
    ctx = ("half", "pair", "core")
    tokens = P("dp", ctx, None)
    return jax.shard_map(
        per_device,
        mesh=fine,
        in_specs=(tokens, tokens, tokens, P(), tokens, P("dp", None)),
        out_specs=(tokens, tokens, tokens, tokens, P(ctx + ("dp",), None)),
        check_vma=False,
    )
```

```python
import jax
import jax.numpy as jnp
from jax import lax
from jax.experimental import pallas as pl
from jax.experimental.pallas import tpu as pltpu
from jax.sharding import Mesh
from jax.sharding import PartitionSpec as P

HDIM = 64
HALVES = 2
CORES = 2
MAXDOC = 1024
CHUNK = 256
STATIC_COUNTS = (2, 3, 4, 5, 6)
VMEM_LIMIT = 60 * 1024 * 1024
SCALE = 0.125
LOG2E = 1.4426950408889634
EXP2_SCALE = SCALE * LOG2E
MASKED = -1e30

f32 = jnp.float32
bf16 = jnp.bfloat16


def mm(a, b):
    return jnp.dot(a, b, preferred_element_type=f32)


def mm_nt(a, b):
    return lax.dot_general(a, b, (((1,), (1,)), ((), ())), preferred_element_type=f32)


def vmem(count):
    return [pl.BlockSpec(memory_space=pltpu.VMEM)] * count


def smem(count):
    return [pl.BlockSpec(memory_space=pltpu.SMEM)] * count


def call(kernel, name, out_shape, in_specs, scratch=(), flops=0, touched=0, *, args):
    many = isinstance(out_shape, tuple)
    return pl.pallas_call(
        kernel,
        out_shape=out_shape,
        in_specs=in_specs,
        out_specs=vmem(len(out_shape)) if many else vmem(1)[0],
        scratch_shapes=list(scratch),
        compiler_params=pltpu.CompilerParams(vmem_limit_bytes=VMEM_LIMIT),
        cost_estimate=pl.CostEstimate(flops=flops, bytes_accessed=touched, transcendentals=0),
        name=name,
    )(*args)


def prep_kernel(q_ref, k_ref, v_ref, len_ref, half_ref, qkv_ref, st_ref, en_ref):
    heads = qkv_ref.shape[0]
    own = st_ref.shape[0] * st_ref.shape[1]
    half = half_ref[0]
    for pair in range(heads // 2):
        cols = slice(pair * 128, pair * 128 + 128)
        for place, source in enumerate((q_ref, k_ref, v_ref)):
            turned = source[:, cols].T
            for side in range(2):
                qkv_ref[2 * pair + side, place * HDIM : place * HDIM + HDIM, :] = turned[
                    side * HDIM : side * HDIM + HDIM
                ]
    shape = st_ref.shape
    position = (
        lax.broadcasted_iota(jnp.int32, shape, 0) * shape[1]
        + lax.broadcasted_iota(jnp.int32, shape, 1)
        + half * own
    )

    def document(index, carry):
        end, begins, ends = carry
        end = end + len_ref[index]
        before = end <= position
        begins = jnp.where(before, end, begins)
        ends = jnp.where(before, ends, jnp.minimum(ends, end))
        return end, begins, ends

    _, begins, ends = lax.fori_loop(
        0,
        len_ref.shape[0],
        document,
        (jnp.int32(0), jnp.zeros(shape, jnp.int32), jnp.full(shape, 2 * own, jnp.int32)),
        unroll=8,
    )
    first = half * (own - MAXDOC)
    st_ref[...] = begins - first
    en_ref[...] = ends - first


def project_kernel(g_ref, w_ref, da_ref):
    grad = g_ref[...]
    for four in range(da_ref.shape[0] // 4):
        part = mm_nt(w_ref[four * 256 : four * 256 + 256, :], grad).astype(bf16)
        for n in range(4):
            da_ref[4 * four + n] = part[n * HDIM : n * HDIM + HDIM]


def span(lo_ref, hi_ref, index):
    low = (lo_ref[index] // 128) * 128
    return low, (hi_ref[index] - low + CHUNK - 1) // CHUNK


def by_count(low, count, total, run):
    for fixed in STATIC_COUNTS:
        here = count == fixed if fixed > STATIC_COUNTS[0] else count <= fixed

        @pl.when(here)
        def _(fixed=fixed):
            run(jnp.minimum(low, total - fixed * CHUNK), fixed)

    @pl.when(count > STATIC_COUNTS[-1])
    def _():
        run(jnp.minimum(low, total - count * CHUNK), count)


def over(count, body, carry):
    if isinstance(count, int):
        for chunk in range(count):
            carry = body(chunk, carry)
        return carry
    return lax.fori_loop(0, count, body, carry)


def chunk_rows(chunk):
    start = chunk * CHUNK
    return pl.ds(start if isinstance(chunk, int) else pl.multiple_of(start, CHUNK), CHUNK)


def forward_kernel(
    half_ref, lo_ref, hi_ref, st_ref, en_ref, qkv_ref, halo_ref,
    attn_ref, stat_ref, kv_n, k_t, v_t, probs,
):
    blocks, _, rows = qkv_ref.shape
    edges = halo_ref.shape[0]
    half = half_ref[0]
    total = kv_n.shape[0]

    def place(block, at):
        at = pl.multiple_of(at, rows)
        k_t[:, pl.ds(at, rows)] = block[:HDIM]
        v_t[:, pl.ds(at, rows)] = block[HDIM:]
        kv_n[pl.ds(at, rows), :] = block.T

    @pl.loop(0, blocks)
    def _(index):
        place(qkv_ref[index, HDIM:, :], half * MAXDOC + index * rows)

    @pl.loop(0, edges)
    def _(index):
        place(halo_ref[index], (1 - half) * blocks * rows + index * rows)

    offset = lax.broadcasted_iota(jnp.int32, (CHUNK, rows), 0)

    @pl.loop(0, blocks)
    def _(index):
        query = qkv_ref[index, :HDIM, :]
        query = jnp.concatenate([query, jnp.zeros_like(query)], axis=0)
        begin = st_ref[pl.ds(index, 1), :]
        length = (en_ref[pl.ds(index, 1), :] - begin).astype(jnp.uint32)

        def run(low, count):
            def at(chunk):
                return pl.multiple_of(low + chunk * CHUNK, 128)

            def score(chunk, top):
                base = at(chunk)
                scores = mm(kv_n[pl.ds(base, CHUNK), :], query)
                inside = (offset - (begin - base)).astype(jnp.uint32) < length
                scores = jnp.where(inside, scores, MASKED)
                probs[chunk_rows(chunk), :] = scores
                return jnp.maximum(top, jnp.max(scores.reshape(CHUNK // 8, 8, rows), axis=0))

            top = over(count, score, jnp.full((8, rows), MASKED, f32))
            top = jnp.max(top, axis=0, keepdims=True)

            def weigh(chunk, carry):
                sums, out = carry
                weights = jnp.exp2((probs[chunk_rows(chunk), :] - top) * EXP2_SCALE)
                sums = sums + jnp.sum(weights.reshape(CHUNK // 8, 8, rows), axis=0)
                out = out + mm(v_t[:, pl.ds(at(chunk), CHUNK)], weights.astype(bf16))
                return sums, out

            sums, out = over(
                count, weigh, (jnp.zeros((8, rows), f32), jnp.zeros((HDIM, rows), f32))
            )
            sums = jnp.sum(sums, axis=0, keepdims=True)
            attn = (out * (1.0 / sums)).astype(bf16)
            attn_ref[index, :HDIM, :] = attn
            side = HDIM // CORES
            sibling = index + 1 - 2 * (index % CORES)
            attn_ref[sibling, HDIM:, :] = jnp.where(
                index % CORES == 0, attn[side:], attn[:side]
            )
            stat_ref[pl.ds(index, 1), :] = top * EXP2_SCALE + jnp.log(sums) * LOG2E

        low, count = span(lo_ref, hi_ref, index)
        by_count(low, count, total, run)


def backward_kernel(
    half_ref, lo_ref, hi_ref, st_ref, en_ref, qkv_ref, da_ref, attn_ref, stat_ref, kv_n, k_t,
    grads_ref, edge_ref, dhalo_ref, acc,
):
    blocks, _, rows = qkv_ref.shape
    edges = edge_ref.shape[0]
    half = half_ref[0]
    total = kv_n.shape[0]

    @pl.loop(0, total // CHUNK)
    def _(chunk):
        acc[:, chunk_rows(chunk)] = jnp.zeros((acc.shape[0], CHUNK), f32)

    offset = lax.broadcasted_iota(jnp.int32, (CHUNK, rows), 0)

    @pl.loop(0, blocks)
    def _(index):
        query_t = qkv_ref[index, :HDIM, :]
        grad_t = da_ref[index]
        nothing = jnp.zeros_like(query_t)
        query = jnp.concatenate([query_t, nothing], axis=0)
        grad = jnp.concatenate([nothing, grad_t], axis=0)
        begin = st_ref[pl.ds(index, 1), :]
        length = (en_ref[pl.ds(index, 1), :] - begin).astype(jnp.uint32)
        log_total = stat_ref[pl.ds(index, 1), :]
        delta = jnp.sum(
            attn_ref[index, :HDIM, :].astype(f32) * grad_t.astype(f32), axis=0, keepdims=True
        )

        def run(low, count):
            def place(chunk):
                return pl.multiple_of(low + chunk * CHUNK, 128)

            def products(chunk):
                both = kv_n[pl.ds(place(chunk), CHUNK), :]
                return mm(both, query), mm(both, grad)

            def derive(chunk, scores, d_probs, d_query):
                base = place(chunk)
                keys = pl.ds(base, CHUNK)
                inside = (offset - (begin - base)).astype(jnp.uint32) < length
                likely = jnp.exp2(jnp.where(inside, scores * EXP2_SCALE - log_total, MASKED))
                d_scores = (likely * (d_probs - delta)).astype(bf16)
                acc[:HDIM, keys] += mm_nt(query_t, d_scores)
                acc[HDIM:, keys] += mm_nt(grad_t, likely.astype(bf16))
                return d_query + mm(k_t[:, keys], d_scores)

            d_query = jnp.zeros((HDIM, rows), f32)
            if isinstance(count, int):
                ahead = products(0)
                for chunk in range(count):
                    scores, d_probs = ahead
                    if chunk + 1 < count:
                        ahead = products(chunk + 1)
                    d_query = derive(chunk, scores, d_probs, d_query)
            else:
                d_query = lax.fori_loop(
                    0, count, lambda chunk, sums: derive(chunk, *products(chunk), sums), d_query
                )
            grads_ref[index, :HDIM, :] = (d_query * SCALE).astype(bf16)

        low, count = span(lo_ref, hi_ref, index)
        by_count(low, count, total, run)

    feature = lax.broadcasted_iota(jnp.int32, (2 * HDIM, rows), 0)
    factor = jnp.where(feature < HDIM, SCALE, 1.0)
    own_at = half * MAXDOC

    @pl.loop(0, blocks)
    def _(index):
        at = pl.multiple_of(own_at + index * rows, rows)
        grads_ref[index, HDIM:, :] = (acc[:, pl.ds(at, rows)] * factor).astype(bf16)

    @pl.loop(0, edges)
    def _(index):
        at = pl.multiple_of((1 - half) * blocks * rows + index * rows, rows)
        dhalo_ref[index] = (acc[:, pl.ds(at, rows)] * factor).astype(bf16)
        at = pl.multiple_of(own_at + (1 - half) * (blocks - edges) * rows + index * rows, rows)
        edge_ref[index] = acc[:, pl.ds(at, rows)] * factor


def weight_kernel(core_ref, attn_ref, g_ref, sibling_ref, out_ref):
    grad, sibling_grad = g_ref[...], sibling_ref[...]
    mine = core_ref[0] == 0
    side = HDIM // CORES
    dp_count, heads = out_ref.shape[:2]
    size = side // dp_count
    own, sibling = [], []
    for head in range(heads):
        rows = attn_ref[head, :HDIM, :]
        own.append(jnp.where(mine, rows[:side], rows[side:]))
        sibling.append(attn_ref[head, HDIM:, :])
    for part in range(2):
        some = slice(part * heads // 2, (part + 1) * heads // 2)
        total = mm(jnp.concatenate(own[some], axis=0), grad)
        total += mm(jnp.concatenate(sibling[some], axis=0), sibling_grad)
        for n, head in enumerate(range(heads)[some]):
            for place in range(dp_count):
                at = n * side + place * size
                out_ref[place, head] = total[at : at + size].astype(bf16)


def output_kernel(attn_ref, w_ref, out_ref):
    parts = [
        jnp.concatenate(
            [attn_ref[2 * pair + side, :HDIM, :] for side in range(2)], axis=0
        ).T
        for pair in range(attn_ref.shape[0] // 2)
    ]
    out_ref[...] = mm(jnp.concatenate(parts, axis=1), w_ref[...]).astype(bf16)


def split_kernel(grads_ref, dq_ref, dk_ref, dv_ref):
    for pair in range(grads_ref.shape[0] // 2):
        cols = slice(pair * 128, pair * 128 + 128)
        for place, target in enumerate((dq_ref, dk_ref, dv_ref)):
            rows = slice(place * HDIM, place * HDIM + HDIM)
            both = [grads_ref[2 * pair + side, rows, :] for side in range(2)]
            target[:, cols] = jnp.concatenate(both, axis=0).T


def per_device(queries, keys, values, w_out, d_out, lengths):
    rows, width = queries.shape[1:]
    group = ("pair", "core")
    blocks = lax.axis_size(group)
    heads = width // HDIM
    edges = MAXDOC // rows
    half = lax.axis_index("half")
    half_scalar = half.reshape(1).astype(jnp.int32)
    side = HDIM // CORES
    dp_count = lax.axis_size("dp")
    core_scalar = lax.axis_index("core").reshape(1).astype(jnp.int32)
    total = blocks * rows + MAXDOC
    most = MAXDOC * 2 + rows + CHUNK
    shape = jax.ShapeDtypeStruct
    swap = [(0, 1), (1, 0)]

    qkv, begins, ends = call(
        prep_kernel,
        "prep",
        (shape((heads, 3 * HDIM, rows), bf16),) + (shape((blocks, rows), jnp.int32),) * 2,
        vmem(3) + smem(2),
        args=(queries[0], keys[0], values[0], lengths[0], half_scalar),
    )
    lows, highs = begins[:, 0], ends[:, rows - 1]
    d_attn = call(
        project_kernel,
        "project",
        shape((heads, HDIM, rows), bf16),
        vmem(2),
        flops=2 * rows * width * width,
        touched=2 * width * width,
        args=(d_out[0], w_out),
    )
    sibling_grad = lax.ppermute(d_out[0], "core", swap)
    qkv = lax.all_to_all(qkv, group, 0, 0, tiled=True)
    qkv, d_attn = lax.optimization_barrier((qkv, d_attn))
    near = lax.dynamic_slice_in_dim(qkv, (1 - half) * (blocks - edges), edges, 0)[:, HDIM:]
    halo = lax.ppermute(near, "half", swap)
    d_attn = lax.all_to_all(d_attn, group, 0, 0, tiled=True)

    attn, stats, kv_n, k_t = call(
        forward_kernel,
        "forward",
        (
            shape((blocks, HDIM + side, rows), bf16),
            shape((blocks, rows), f32),
            shape((total, 2 * HDIM), bf16),
            shape((HDIM, total), bf16),
        ),
        smem(3) + vmem(4),
        (pltpu.VMEM((HDIM, total), bf16), pltpu.VMEM((most, rows), f32)),
        flops=10**10,
        touched=10**7,
        args=(half_scalar, lows, highs, begins, ends, qkv, halo),
    )
    grads, edge, dhalo = call(
        backward_kernel,
        "backward",
        (
            shape((blocks, 3 * HDIM, rows), bf16),
            shape((edges, 2 * HDIM, rows), f32),
            shape((edges, 2 * HDIM, rows), bf16),
        ),
        smem(3) + vmem(8),
        (pltpu.VMEM((2 * HDIM, total), f32),),
        flops=10**10,
        touched=10**7,
        args=(half_scalar, lows, highs, begins, ends, qkv, d_attn, attn, stats, kv_n, k_t),
    )
    attn = lax.all_to_all(attn, group, 0, 0, tiled=True)
    dhalo = lax.ppermute(dhalo, "half", swap)
    attn, grads, edge = lax.optimization_barrier((attn, grads, edge))
    chip_sum = call(
        weight_kernel,
        "weight",
        shape((dp_count, heads, side // dp_count, width), bf16),
        smem(1) + vmem(3),
        flops=2 * rows * width * width,
        touched=4 * width * width,
        args=(core_scalar, attn, d_out[0], sibling_grad),
    )
    dhalo, chip_sum = lax.optimization_barrier((dhalo, chip_sum))
    mine = lax.axis_index("dp")
    column = lax.dynamic_index_in_dim(chip_sum, mine, 0, keepdims=False).astype(f32)
    for step in range(1, dp_count):
        part = lax.dynamic_index_in_dim(chip_sum, (mine + step) % dp_count, 0, keepdims=False)
        moves = [(d, (d + step) % dp_count) for d in range(dp_count)]
        column = column + lax.ppermute(part, "dp", moves).astype(f32)

    edge = (edge + dhalo.astype(f32)).astype(bf16)
    grads = lax.dynamic_update_slice(grads, edge, ((1 - half) * (blocks - edges), HDIM, 0))
    grads = lax.all_to_all(grads, group, 0, 0, tiled=True)
    column, grads = lax.optimization_barrier((column.astype(bf16), grads))
    parts = lax.all_to_all(column, ("half", "pair"), 0, 0, tiled=True)
    w_grad = jnp.sum(parts.astype(f32), axis=0)

    flat = shape((rows, width), bf16)
    output = call(
        output_kernel,
        "output",
        flat,
        vmem(2),
        flops=2 * rows * width * width,
        touched=2 * width * width,
        args=(attn, w_out),
    )
    d_queries, d_keys, d_values = call(
        split_kernel, "split", (flat,) * 3, vmem(1), args=(grads,)
    )
    return (output[None], d_queries[None], d_keys[None], d_values[None], w_grad)


def solution(mesh):
    ctx_count, dp_count = mesh.devices.shape
    pairs = ctx_count // (HALVES * CORES)
    fine = Mesh(
        mesh.devices.reshape(HALVES, pairs, CORES, dp_count), ("half", "pair", "core", "dp")
    )
    ctx = ("half", "pair", "core")
    tokens = P("dp", ctx, None)
    return jax.shard_map(
        per_device,
        mesh=fine,
        in_specs=(tokens, tokens, tokens, P(), tokens, P("dp", None)),
        out_specs=(tokens, tokens, tokens, tokens, P(ctx + ("dp",), None)),
        check_vma=False,
    )
```

```python
import jax
import jax.numpy as jnp
from jax import lax
from jax.experimental import pallas as pl
from jax.experimental.pallas import tpu as pltpu
from jax.sharding import Mesh
from jax.sharding import PartitionSpec as P

HDIM = 64
HALVES = 2
CORES = 2
MAXDOC = 1024
CHUNK = 256
STEP = 128
STATIC_COUNTS = (2, 3, 4, 5, 6)
TOGETHER = 2
VMEM_LIMIT = 60 * 1024 * 1024
SCALE = 0.125
LOG2E = 1.4426950408889634
EXP2_SCALE = SCALE * LOG2E
MASKED = -1e30

f32 = jnp.float32
bf16 = jnp.bfloat16


def mm(a, b):
    return jnp.dot(a, b, preferred_element_type=f32)


def mm_nt(a, b):
    return lax.dot_general(a, b, (((1,), (1,)), ((), ())), preferred_element_type=f32)


def vmem(count):
    return [pl.BlockSpec(memory_space=pltpu.VMEM)] * count


def smem(count):
    return [pl.BlockSpec(memory_space=pltpu.SMEM)] * count


def call(kernel, name, out_shape, in_specs, scratch=(), flops=0, touched=0, *, args):
    many = isinstance(out_shape, tuple)
    return pl.pallas_call(
        kernel,
        out_shape=out_shape,
        in_specs=in_specs,
        out_specs=vmem(len(out_shape)) if many else vmem(1)[0],
        scratch_shapes=list(scratch),
        compiler_params=pltpu.CompilerParams(vmem_limit_bytes=VMEM_LIMIT),
        cost_estimate=pl.CostEstimate(flops=flops, bytes_accessed=touched, transcendentals=0),
        name=name,
    )(*args)


def prep_kernel(q_ref, k_ref, v_ref, len_ref, half_ref, qkv_ref, st_ref, en_ref):
    heads = qkv_ref.shape[0]
    own = st_ref.shape[0] * st_ref.shape[1]
    half = half_ref[0]
    for pair in range(heads // 2):
        cols = slice(pair * 128, pair * 128 + 128)
        for place, source in enumerate((q_ref, k_ref, v_ref)):
            turned = source[:, cols].T
            for side in range(2):
                qkv_ref[2 * pair + side, place * HDIM : place * HDIM + HDIM, :] = turned[
                    side * HDIM : side * HDIM + HDIM
                ]
    shape = st_ref.shape
    position = (
        lax.broadcasted_iota(jnp.int32, shape, 0) * shape[1]
        + lax.broadcasted_iota(jnp.int32, shape, 1)
        + half * own
    )

    def document(index, carry):
        end, begins, ends = carry
        end = end + len_ref[index]
        before = end <= position
        begins = jnp.where(before, end, begins)
        ends = jnp.where(before, ends, jnp.minimum(ends, end))
        return end, begins, ends

    _, begins, ends = lax.fori_loop(
        0,
        len_ref.shape[0],
        document,
        (jnp.int32(0), jnp.zeros(shape, jnp.int32), jnp.full(shape, 2 * own, jnp.int32)),
        unroll=8,
    )
    first = half * (own - MAXDOC)
    st_ref[...] = begins - first
    en_ref[...] = ends - first


def project_kernel(g_ref, w_ref, da_ref):
    grad = g_ref[...]
    for four in range(da_ref.shape[0] // 4):
        part = mm_nt(w_ref[four * 256 : four * 256 + 256, :], grad).astype(bf16)
        for n in range(4):
            da_ref[4 * four + n] = part[n * HDIM : n * HDIM + HDIM]


def span(lo_ref, hi_ref, index):
    low = (lo_ref[index] // STEP) * STEP
    return low, (hi_ref[index] - low + CHUNK - 1) // CHUNK


def by_count(lo_ref, hi_ref, total, order, tally, run):
    blocks = lo_ref.shape[0]
    least, kinds = STATIC_COUNTS[0], len(STATIC_COUNTS) + 1

    def kind_of(index):
        return jnp.clip(span(lo_ref, hi_ref, index)[1] - least, 0, kinds - 1)

    for kind in range(kinds):
        tally[kind] = 0

    @pl.loop(0, blocks)
    def _(index):
        kind = kind_of(index)
        tally[kind] = tally[kind] + 1

    ends, end = [], 0
    for kind in range(kinds):
        begin, end = end, end + tally[kind]
        tally[kind] = begin
        ends.append(end)

    @pl.loop(0, blocks)
    def _(index):
        kind = kind_of(index)
        place = tally[kind]
        tally[kind] = place + 1
        order[place] = index

    begin = 0
    for kind, end in enumerate(ends):

        @pl.loop(begin // TOGETHER, end // TOGETHER)
        def _(place, kind=kind):
            members = [order[place * TOGETHER + n] for n in range(TOGETHER)]
            spans = [span(lo_ref, hi_ref, index) for index in members]
            if kind < kinds - 1:
                count = STATIC_COUNTS[kind]
            else:
                count = spans[0][1]
                for _, other in spans[1:]:
                    count = jnp.maximum(count, other)
            lows = [jnp.minimum(low, total - count * CHUNK) for low, _ in spans]
            run(members, lows, count)

        begin = end


def over(count, body, carry):
    if isinstance(count, int):
        for chunk in range(count):
            carry = body(chunk * CHUNK, carry)
        return carry
    return lax.fori_loop(
        0, count, lambda chunk, c: body(pl.multiple_of(chunk * CHUNK, CHUNK), c), carry
    )


def forward_kernel(
    half_ref, lo_ref, hi_ref, st_ref, en_ref, qkv_ref, halo_ref,
    attn_ref, stat_ref, kv_n, k_t, v_t, probs, order, tally,
):
    blocks, _, rows = qkv_ref.shape
    edges = halo_ref.shape[0]
    half = half_ref[0]
    total = kv_n.shape[0]

    def place(block, at):
        at = pl.multiple_of(at, rows)
        k_t[:, pl.ds(at, rows)] = block[:HDIM]
        v_t[:, pl.ds(at, rows)] = block[HDIM:]
        kv_n[pl.ds(at, rows), :] = block.T

    for index in range(blocks):
        place(qkv_ref[index, HDIM:, :], half * MAXDOC + index * rows)
    for index in range(edges):
        place(halo_ref[index], (1 - half) * blocks * rows + index * rows)

    offset = lax.broadcasted_iota(jnp.int32, (CHUNK, rows), 0)

    def run(members, lows, count):
        many = range(len(members))
        queries, begins, lengths = [], [], []
        for index in members:
            query = qkv_ref[index, :HDIM, :]
            queries.append(jnp.concatenate([query, jnp.zeros_like(query)], axis=0))
            begins.append(st_ref[pl.ds(index, 1), :])
            lengths.append((en_ref[pl.ds(index, 1), :] - begins[-1]).astype(jnp.uint32))

        def score(start, tops):
            news = []
            for n in many:
                base = pl.multiple_of(lows[n] + start, STEP)
                scores = mm(kv_n[pl.ds(base, CHUNK), :], queries[n])
                inside = (offset - (begins[n] - base)).astype(jnp.uint32) < lengths[n]
                scores = jnp.where(inside, scores, MASKED)
                probs[n, pl.ds(start, CHUNK), :] = scores
                most = jnp.max(scores.reshape(CHUNK // 8, 8, rows), axis=0)
                news.append(jnp.maximum(tops[n], most))
            return news

        tops = over(count, score, [jnp.full((8, rows), MASKED, f32)] * len(members))
        tops = [jnp.max(top, axis=0, keepdims=True) for top in tops]

        def weigh(start, carry):
            news = []
            for n in many:
                sums, out = carry[n]
                keys = pl.ds(pl.multiple_of(lows[n] + start, STEP), CHUNK)
                weights = jnp.exp2((probs[n, pl.ds(start, CHUNK), :] - tops[n]) * EXP2_SCALE)
                sums = sums + jnp.sum(weights.reshape(CHUNK // 8, 8, rows), axis=0)
                news.append((sums, out + mm(v_t[:, keys], weights.astype(bf16))))
            return news

        nothing = (jnp.zeros((8, rows), f32), jnp.zeros((HDIM, rows), f32))
        totals = over(count, weigh, [nothing] * len(members))
        for index, top, (sums, out) in zip(members, tops, totals):
            sums = jnp.sum(sums, axis=0, keepdims=True)
            attn = (out * (1.0 / sums)).astype(bf16)
            attn_ref[index, :HDIM, :] = attn
            side = HDIM // CORES
            sibling = index + 1 - 2 * (index % CORES)
            attn_ref[sibling, HDIM:, :] = jnp.where(
                index % CORES == 0, attn[side:], attn[:side]
            )
            stat_ref[pl.ds(index, 1), :] = top * EXP2_SCALE + jnp.log(sums) * LOG2E

    by_count(lo_ref, hi_ref, total, order, tally, run)


def backward_kernel(
    half_ref, lo_ref, hi_ref, st_ref, en_ref, qkv_ref, da_ref, attn_ref, stat_ref, kv_n, k_t,
    grads_ref, edge_ref, dhalo_ref, acc, order, tally,
):
    blocks, _, rows = qkv_ref.shape
    edges = edge_ref.shape[0]
    half = half_ref[0]
    total = kv_n.shape[0]

    @pl.loop(0, total // CHUNK)
    def _(chunk):
        keys = pl.ds(pl.multiple_of(chunk * CHUNK, CHUNK), CHUNK)
        acc[:, keys] = jnp.zeros((acc.shape[0], CHUNK), f32)

    offset = lax.broadcasted_iota(jnp.int32, (CHUNK, rows), 0)

    def run(members, lows, count):
        fixed = []
        for index in members:
            query_t = qkv_ref[index, :HDIM, :]
            grad_t = da_ref[index]
            nothing = jnp.zeros_like(query_t)
            begin = st_ref[pl.ds(index, 1), :]
            attn = attn_ref[index, :HDIM, :].astype(f32)
            fixed.append(
                dict(
                    query_t=query_t,
                    grad_t=grad_t,
                    query=jnp.concatenate([query_t, nothing], axis=0),
                    grad=jnp.concatenate([nothing, grad_t], axis=0),
                    begin=begin,
                    length=(en_ref[pl.ds(index, 1), :] - begin).astype(jnp.uint32),
                    log_total=stat_ref[pl.ds(index, 1), :],
                    delta=jnp.sum(attn * grad_t.astype(f32), axis=0, keepdims=True),
                )
            )

        def products(n, start):
            both = kv_n[pl.ds(pl.multiple_of(lows[n] + start, STEP), CHUNK), :]
            return mm(both, fixed[n]["query"]), mm(both, fixed[n]["grad"])

        def derive(n, start, scores, d_probs, d_query):
            own = fixed[n]
            base = pl.multiple_of(lows[n] + start, STEP)
            keys = pl.ds(base, CHUNK)
            inside = (offset - (own["begin"] - base)).astype(jnp.uint32) < own["length"]
            exponent = scores * EXP2_SCALE - own["log_total"]
            likely = jnp.exp2(jnp.where(inside, exponent, MASKED))
            d_scores = (likely * (d_probs - own["delta"])).astype(bf16)
            acc[:HDIM, keys] += mm_nt(own["query_t"], d_scores)
            acc[HDIM:, keys] += mm_nt(own["grad_t"], likely.astype(bf16))
            return d_query + mm(k_t[:, keys], d_scores)

        d_queries = [jnp.zeros((HDIM, rows), f32)] * len(members)
        if isinstance(count, int):
            items = [(n, c * CHUNK) for c in range(count) for n in range(len(members))]
            ahead = products(*items[0])
            for (n, start), after in zip(items, items[1:] + [None]):
                now = ahead
                if after is not None:
                    ahead = products(*after)
                d_queries[n] = derive(n, start, *now, d_queries[n])
        else:

            def step(start, sums):
                return [
                    derive(n, start, *products(n, start), sums[n]) for n in range(len(members))
                ]

            d_queries = over(count, step, d_queries)
        for index, d_query in zip(members, d_queries):
            grads_ref[index, :HDIM, :] = (d_query * SCALE).astype(bf16)

    by_count(lo_ref, hi_ref, total, order, tally, run)

    feature = lax.broadcasted_iota(jnp.int32, (2 * HDIM, rows), 0)
    factor = jnp.where(feature < HDIM, SCALE, 1.0)
    own_at = half * MAXDOC

    @pl.loop(0, blocks)
    def _(index):
        at = pl.multiple_of(own_at + index * rows, rows)
        grads_ref[index, HDIM:, :] = (acc[:, pl.ds(at, rows)] * factor).astype(bf16)

    @pl.loop(0, edges)
    def _(index):
        at = pl.multiple_of((1 - half) * blocks * rows + index * rows, rows)
        dhalo_ref[index] = (acc[:, pl.ds(at, rows)] * factor).astype(bf16)
        at = pl.multiple_of(own_at + (1 - half) * (blocks - edges) * rows + index * rows, rows)
        edge_ref[index] = acc[:, pl.ds(at, rows)] * factor


def weight_kernel(core_ref, attn_ref, g_ref, sibling_ref, out_ref):
    grad, sibling_grad = g_ref[...], sibling_ref[...]
    mine = core_ref[0] == 0
    side = HDIM // CORES
    dp_count, heads = out_ref.shape[:2]
    size = side // dp_count
    own, sibling = [], []
    for head in range(heads):
        rows = attn_ref[head, :HDIM, :]
        own.append(jnp.where(mine, rows[:side], rows[side:]))
        sibling.append(attn_ref[head, HDIM:, :])
    for part in range(2):
        some = slice(part * heads // 2, (part + 1) * heads // 2)
        total = mm(jnp.concatenate(own[some], axis=0), grad)
        total += mm(jnp.concatenate(sibling[some], axis=0), sibling_grad)
        for n, head in enumerate(range(heads)[some]):
            for place in range(dp_count):
                at = n * side + place * size
                out_ref[place, head] = total[at : at + size].astype(bf16)


def output_kernel(attn_ref, w_ref, out_ref):
    parts = [
        jnp.concatenate(
            [attn_ref[2 * pair + side, :HDIM, :] for side in range(2)], axis=0
        ).T
        for pair in range(attn_ref.shape[0] // 2)
    ]
    out_ref[...] = mm(jnp.concatenate(parts, axis=1), w_ref[...]).astype(bf16)


def split_kernel(grads_ref, dq_ref, dk_ref, dv_ref):
    for pair in range(grads_ref.shape[0] // 2):
        cols = slice(pair * 128, pair * 128 + 128)
        for place, target in enumerate((dq_ref, dk_ref, dv_ref)):
            rows = slice(place * HDIM, place * HDIM + HDIM)
            both = [grads_ref[2 * pair + side, rows, :] for side in range(2)]
            target[:, cols] = jnp.concatenate(both, axis=0).T


def per_device(queries, keys, values, w_out, d_out, lengths):
    rows, width = queries.shape[1:]
    group = ("pair", "core")
    blocks = lax.axis_size(group)
    heads = width // HDIM
    edges = MAXDOC // rows
    half = lax.axis_index("half")
    half_scalar = half.reshape(1).astype(jnp.int32)
    side = HDIM // CORES
    dp_count = lax.axis_size("dp")
    core_scalar = lax.axis_index("core").reshape(1).astype(jnp.int32)
    total = blocks * rows + MAXDOC
    most = MAXDOC * 2 + rows + CHUNK
    shape = jax.ShapeDtypeStruct
    lists = (pltpu.SMEM((blocks,), jnp.int32), pltpu.SMEM((8,), jnp.int32))
    swap = [(0, 1), (1, 0)]

    qkv, begins, ends = call(
        prep_kernel,
        "prep",
        (shape((heads, 3 * HDIM, rows), bf16),) + (shape((blocks, rows), jnp.int32),) * 2,
        vmem(3) + smem(2),
        args=(queries[0], keys[0], values[0], lengths[0], half_scalar),
    )
    lows, highs = begins[:, 0], ends[:, rows - 1]
    d_attn = call(
        project_kernel,
        "project",
        shape((heads, HDIM, rows), bf16),
        vmem(2),
        flops=2 * rows * width * width,
        touched=2 * width * width,
        args=(d_out[0], w_out),
    )
    sibling_grad = lax.ppermute(d_out[0], "core", swap)
    qkv = lax.all_to_all(qkv, group, 0, 0, tiled=True)
    qkv, d_attn = lax.optimization_barrier((qkv, d_attn))
    near = lax.dynamic_slice_in_dim(qkv, (1 - half) * (blocks - edges), edges, 0)[:, HDIM:]
    halo = lax.ppermute(near, "half", swap)
    d_attn = lax.all_to_all(d_attn, group, 0, 0, tiled=True)

    attn, stats, kv_n, k_t = call(
        forward_kernel,
        "forward",
        (
            shape((blocks, HDIM + side, rows), bf16),
            shape((blocks, rows), f32),
            shape((total, 2 * HDIM), bf16),
            shape((HDIM, total), bf16),
        ),
        smem(3) + vmem(4),
        (pltpu.VMEM((HDIM, total), bf16), pltpu.VMEM((TOGETHER, most, rows), f32)) + lists,
        flops=10**10,
        touched=10**7,
        args=(half_scalar, lows, highs, begins, ends, qkv, halo),
    )
    grads, edge, dhalo = call(
        backward_kernel,
        "backward",
        (
            shape((blocks, 3 * HDIM, rows), bf16),
            shape((edges, 2 * HDIM, rows), f32),
            shape((edges, 2 * HDIM, rows), bf16),
        ),
        smem(3) + vmem(8),
        (pltpu.VMEM((2 * HDIM, total), f32),) + lists,
        flops=10**10,
        touched=10**7,
        args=(half_scalar, lows, highs, begins, ends, qkv, d_attn, attn, stats, kv_n, k_t),
    )
    attn = lax.all_to_all(attn, group, 0, 0, tiled=True)
    dhalo = lax.ppermute(dhalo, "half", swap)
    attn, grads, edge = lax.optimization_barrier((attn, grads, edge))
    chip_sum = call(
        weight_kernel,
        "weight",
        shape((dp_count, heads, side // dp_count, width), bf16),
        smem(1) + vmem(3),
        flops=2 * rows * width * width,
        touched=4 * width * width,
        args=(core_scalar, attn, d_out[0], sibling_grad),
    )
    dhalo, chip_sum = lax.optimization_barrier((dhalo, chip_sum))
    mine = lax.axis_index("dp")
    column = lax.dynamic_index_in_dim(chip_sum, mine, 0, keepdims=False).astype(f32)
    for step in range(1, dp_count):
        part = lax.dynamic_index_in_dim(chip_sum, (mine + step) % dp_count, 0, keepdims=False)
        moves = [(d, (d + step) % dp_count) for d in range(dp_count)]
        column = column + lax.ppermute(part, "dp", moves).astype(f32)

    edge = (edge + dhalo.astype(f32)).astype(bf16)
    grads = lax.dynamic_update_slice(grads, edge, ((1 - half) * (blocks - edges), HDIM, 0))
    grads = lax.all_to_all(grads, group, 0, 0, tiled=True)
    column, grads = lax.optimization_barrier((column.astype(bf16), grads))
    parts = lax.all_to_all(column, ("half", "pair"), 0, 0, tiled=True)
    w_grad = jnp.sum(parts.astype(f32), axis=0)

    flat = shape((rows, width), bf16)
    output = call(
        output_kernel,
        "output",
        flat,
        vmem(2),
        flops=2 * rows * width * width,
        touched=2 * width * width,
        args=(attn, w_out),
    )
    d_queries, d_keys, d_values = call(
        split_kernel, "split", (flat,) * 3, vmem(1), args=(grads,)
    )
    return (output[None], d_queries[None], d_keys[None], d_values[None], w_grad)


def solution(mesh):
    ctx_count, dp_count = mesh.devices.shape
    pairs = ctx_count // (HALVES * CORES)
    fine = Mesh(
        mesh.devices.reshape(HALVES, pairs, CORES, dp_count), ("half", "pair", "core", "dp")
    )
    ctx = ("half", "pair", "core")
    tokens = P("dp", ctx, None)
    return jax.shard_map(
        per_device,
        mesh=fine,
        in_specs=(tokens, tokens, tokens, P(), tokens, P("dp", None)),
        out_specs=(tokens, tokens, tokens, tokens, P(ctx + ("dp",), None)),
        check_vma=False,
    )
```

```python
import jax
import jax.numpy as jnp
from jax import lax
from jax.experimental import pallas as pl
from jax.experimental.pallas import tpu as pltpu
from jax.sharding import Mesh
from jax.sharding import PartitionSpec as P

HDIM = 64
HALVES = 2
CORES = 2
MAXDOC = 1024
CHUNK = 256
STEP = 128
STATIC_COUNTS = (2, 3, 4, 5, 6)
TOGETHER = 2
AHEAD = 2
VMEM_LIMIT = 60 * 1024 * 1024
SCALE = 0.125
LOG2E = 1.4426950408889634
EXP2_SCALE = SCALE * LOG2E
MASKED = -1e30

f32 = jnp.float32
bf16 = jnp.bfloat16


def mm(a, b):
    return jnp.dot(a, b, preferred_element_type=f32)


def mm_nt(a, b):
    return lax.dot_general(a, b, (((1,), (1,)), ((), ())), preferred_element_type=f32)


def vmem(count):
    return [pl.BlockSpec(memory_space=pltpu.VMEM)] * count


def smem(count):
    return [pl.BlockSpec(memory_space=pltpu.SMEM)] * count


def call(kernel, name, out_shape, in_specs, scratch=(), flops=0, touched=0, grid=(), *, args):
    many = isinstance(out_shape, tuple)
    return pl.pallas_call(
        kernel,
        out_shape=out_shape,
        grid=grid,
        in_specs=in_specs,
        out_specs=vmem(len(out_shape)) if many else vmem(1)[0],
        scratch_shapes=list(scratch),
        compiler_params=pltpu.CompilerParams(vmem_limit_bytes=VMEM_LIMIT),
        cost_estimate=pl.CostEstimate(flops=flops, bytes_accessed=touched, transcendentals=0),
        name=name,
    )(*args)


def prep_kernel(q_ref, k_ref, v_ref, len_ref, half_ref, qkv_ref, st_ref, en_ref):
    heads = qkv_ref.shape[0]
    own = st_ref.shape[0] * st_ref.shape[1]
    half = half_ref[0]
    for pair in range(heads // 2):
        cols = slice(pair * 128, pair * 128 + 128)
        for place, source in enumerate((q_ref, k_ref, v_ref)):
            turned = source[:, cols].T
            for side in range(2):
                qkv_ref[2 * pair + side, place * HDIM : place * HDIM + HDIM, :] = turned[
                    side * HDIM : side * HDIM + HDIM
                ]
    shape = st_ref.shape
    position = (
        lax.broadcasted_iota(jnp.int32, shape, 0) * shape[1]
        + lax.broadcasted_iota(jnp.int32, shape, 1)
        + half * own
    )

    def document(index, carry):
        end, begins, ends = carry
        end = end + len_ref[index]
        before = end <= position
        begins = jnp.where(before, end, begins)
        ends = jnp.where(before, ends, jnp.minimum(ends, end))
        return end, begins, ends

    _, begins, ends = lax.fori_loop(
        0,
        len_ref.shape[0],
        document,
        (jnp.int32(0), jnp.zeros(shape, jnp.int32), jnp.full(shape, 2 * own, jnp.int32)),
        unroll=8,
    )
    first = half * (own - MAXDOC)
    st_ref[...] = begins - first
    en_ref[...] = ends - first


def project_kernel(g_ref, w_ref, da_ref):
    grad = g_ref[...]
    for four in range(da_ref.shape[0] // 4):
        part = mm_nt(w_ref[four * 256 : four * 256 + 256, :], grad).astype(bf16)
        for n in range(4):
            da_ref[4 * four + n] = part[n * HDIM : n * HDIM + HDIM]


def span(lo_ref, hi_ref, index):
    low = (lo_ref[index] // STEP) * STEP
    return low, (hi_ref[index] - low + CHUNK - 1) // CHUNK


def by_count(lo_ref, hi_ref, total, order, tally, run):
    blocks = lo_ref.shape[0]
    least, kinds = STATIC_COUNTS[0], len(STATIC_COUNTS) + 1

    def kind_of(index):
        return jnp.clip(span(lo_ref, hi_ref, index)[1] - least, 0, kinds - 1)

    for kind in range(kinds):
        tally[kind] = 0

    @pl.loop(0, blocks)
    def _(index):
        kind = kind_of(index)
        tally[kind] = tally[kind] + 1

    ends, end = [], 0
    for kind in range(kinds):
        begin, end = end, end + tally[kind]
        tally[kind] = begin
        ends.append(end)

    @pl.loop(0, blocks)
    def _(index):
        kind = kind_of(index)
        place = tally[kind]
        tally[kind] = place + 1
        order[place] = index

    begin = 0
    for kind, end in enumerate(ends):

        @pl.loop(begin // TOGETHER, end // TOGETHER)
        def _(place, kind=kind):
            members = [order[place * TOGETHER + n] for n in range(TOGETHER)]
            spans = [span(lo_ref, hi_ref, index) for index in members]
            if kind < kinds - 1:
                count = STATIC_COUNTS[kind]
            else:
                count = spans[0][1]
                for _, other in spans[1:]:
                    count = jnp.maximum(count, other)
            lows = [jnp.minimum(low, total - count * CHUNK) for low, _ in spans]
            run(members, lows, count)

        begin = end


def over(count, body, carry):
    if isinstance(count, int):
        for chunk in range(count):
            carry = body(chunk * CHUNK, carry)
        return carry
    return lax.fori_loop(
        0, count, lambda chunk, c: body(pl.multiple_of(chunk * CHUNK, CHUNK), c), carry
    )


def forward_kernel(
    half_ref, lo_ref, hi_ref, st_ref, en_ref, qkv_ref, halo_ref,
    attn_ref, stat_ref, kv_n, k_t, v_t, probs, order, tally,
):
    blocks, _, rows = qkv_ref.shape
    edges = halo_ref.shape[0]
    half = half_ref[0]
    total = kv_n.shape[0]

    def place(block, at):
        at = pl.multiple_of(at, rows)
        k_t[:, pl.ds(at, rows)] = block[:HDIM]
        v_t[:, pl.ds(at, rows)] = block[HDIM:]
        kv_n[pl.ds(at, rows), :] = block.T

    for index in range(blocks):
        place(qkv_ref[index, HDIM:, :], half * MAXDOC + index * rows)
    for index in range(edges):
        place(halo_ref[index], (1 - half) * blocks * rows + index * rows)

    offset = lax.broadcasted_iota(jnp.int32, (CHUNK, rows), 0)

    def run(members, lows, count):
        many = range(len(members))
        queries, begins, lengths = [], [], []
        for index in members:
            query = qkv_ref[index, :HDIM, :]
            queries.append(jnp.concatenate([query, jnp.zeros_like(query)], axis=0))
            begins.append(st_ref[pl.ds(index, 1), :])
            lengths.append((en_ref[pl.ds(index, 1), :] - begins[-1]).astype(jnp.uint32))

        def score(start, tops):
            news = []
            for n in many:
                base = pl.multiple_of(lows[n] + start, STEP)
                scores = mm(kv_n[pl.ds(base, CHUNK), :], queries[n])
                inside = (offset - (begins[n] - base)).astype(jnp.uint32) < lengths[n]
                scores = jnp.where(inside, scores, MASKED)
                probs[n, pl.ds(start, CHUNK), :] = scores
                most = jnp.max(scores.reshape(CHUNK // 8, 8, rows), axis=0)
                news.append(jnp.maximum(tops[n], most))
            return news

        tops = over(count, score, [jnp.full((8, rows), MASKED, f32)] * len(members))
        tops = [jnp.max(top, axis=0, keepdims=True) for top in tops]

        def weigh(start, carry):
            news = []
            for n in many:
                sums, out = carry[n]
                keys = pl.ds(pl.multiple_of(lows[n] + start, STEP), CHUNK)
                weights = jnp.exp2((probs[n, pl.ds(start, CHUNK), :] - tops[n]) * EXP2_SCALE)
                sums = sums + jnp.sum(weights.reshape(CHUNK // 8, 8, rows), axis=0)
                news.append((sums, out + mm(v_t[:, keys], weights.astype(bf16))))
            return news

        nothing = (jnp.zeros((8, rows), f32), jnp.zeros((HDIM, rows), f32))
        totals = over(count, weigh, [nothing] * len(members))
        for index, top, (sums, out) in zip(members, tops, totals):
            sums = jnp.sum(sums, axis=0, keepdims=True)
            attn = (out * (1.0 / sums)).astype(bf16)
            attn_ref[index, :HDIM, :] = attn
            side = HDIM // CORES
            sibling = index + 1 - 2 * (index % CORES)
            attn_ref[sibling, HDIM:, :] = jnp.where(
                index % CORES == 0, attn[side:], attn[:side]
            )
            stat_ref[pl.ds(index, 1), :] = top * EXP2_SCALE + jnp.log(sums) * LOG2E

    by_count(lo_ref, hi_ref, total, order, tally, run)


def backward_kernel(
    half_ref, lo_ref, hi_ref, st_ref, en_ref, q_ref, da_ref, attn_ref, stat_ref, kv_n, k_t,
    grads_ref, edge_ref, dhalo_ref, acc, order, tally,
):
    blocks, _, rows = q_ref.shape
    edges = edge_ref.shape[0]
    half = half_ref[0]
    total = kv_n.shape[0]

    @pl.loop(0, total // CHUNK)
    def _(chunk):
        keys = pl.ds(pl.multiple_of(chunk * CHUNK, CHUNK), CHUNK)
        acc[:, keys] = jnp.zeros((acc.shape[0], CHUNK), f32)

    offset = lax.broadcasted_iota(jnp.int32, (CHUNK, rows), 0)

    def run(members, lows, count):
        fixed = []
        for index in members:
            query_t = q_ref[index]
            grad_t = da_ref[index]
            nothing = jnp.zeros_like(query_t)
            begin = st_ref[pl.ds(index, 1), :]
            attn = attn_ref[index].astype(f32)
            fixed.append(
                dict(
                    query_t=query_t,
                    grad_t=grad_t,
                    query=jnp.concatenate([query_t, nothing], axis=0),
                    grad=jnp.concatenate([nothing, grad_t], axis=0),
                    begin=begin,
                    length=(en_ref[pl.ds(index, 1), :] - begin).astype(jnp.uint32),
                    log_total=stat_ref[pl.ds(index, 1), :],
                    delta=jnp.sum(attn * grad_t.astype(f32), axis=0, keepdims=True),
                )
            )

        def products(n, start):
            both = kv_n[pl.ds(pl.multiple_of(lows[n] + start, STEP), CHUNK), :]
            return mm(both, fixed[n]["query"]), mm(both, fixed[n]["grad"])

        def derive(n, start, scores, d_probs, d_query):
            own = fixed[n]
            base = pl.multiple_of(lows[n] + start, STEP)
            keys = pl.ds(base, CHUNK)
            inside = (offset - (own["begin"] - base)).astype(jnp.uint32) < own["length"]
            exponent = scores * EXP2_SCALE - own["log_total"]
            likely = jnp.exp2(jnp.where(inside, exponent, MASKED))
            d_scores = (likely * (d_probs - own["delta"])).astype(bf16)
            acc[:HDIM, keys] += mm_nt(own["query_t"], d_scores)
            acc[HDIM:, keys] += mm_nt(own["grad_t"], likely.astype(bf16))
            return d_query + mm(k_t[:, keys], d_scores)

        d_queries = [jnp.zeros((HDIM, rows), f32)] * len(members)
        if isinstance(count, int):
            items = [(n, c * CHUNK) for c in range(count) for n in range(len(members))]
            ahead = [products(*item) for item in items[:AHEAD]]
            for place, (n, start) in enumerate(items):
                now = ahead.pop(0)
                if place + AHEAD < len(items):
                    ahead.append(products(*items[place + AHEAD]))
                d_queries[n] = derive(n, start, *now, d_queries[n])
        else:

            def step(start, sums):
                return [
                    derive(n, start, *products(n, start), sums[n]) for n in range(len(members))
                ]

            d_queries = over(count, step, d_queries)
        for index, d_query in zip(members, d_queries):
            grads_ref[index, :HDIM, :] = (d_query * SCALE).astype(bf16)

    by_count(lo_ref, hi_ref, total, order, tally, run)

    feature = lax.broadcasted_iota(jnp.int32, (2 * HDIM, rows), 0)
    factor = jnp.where(feature < HDIM, SCALE, 1.0)
    own_at = half * MAXDOC

    @pl.loop(0, blocks)
    def _(index):
        at = pl.multiple_of(own_at + index * rows, rows)
        grads_ref[index, HDIM:, :] = (acc[:, pl.ds(at, rows)] * factor).astype(bf16)

    @pl.loop(0, edges)
    def _(index):
        at = pl.multiple_of((1 - half) * blocks * rows + index * rows, rows)
        dhalo_ref[index] = (acc[:, pl.ds(at, rows)] * factor).astype(bf16)
        at = pl.multiple_of(own_at + (1 - half) * (blocks - edges) * rows + index * rows, rows)
        edge_ref[index] = acc[:, pl.ds(at, rows)] * factor


def weight_kernel(core_ref, attn_ref, g_ref, sibling_ref, out_ref):
    grad, sibling_grad = g_ref[...], sibling_ref[...]
    mine = core_ref[0] == 0
    side = HDIM // CORES
    dp_count, heads = out_ref.shape[:2]
    size = side // dp_count
    own, sibling = [], []
    for head in range(heads):
        rows = attn_ref[head, :HDIM, :]
        own.append(jnp.where(mine, rows[:side], rows[side:]))
        sibling.append(attn_ref[head, HDIM:, :])
    for part in range(2):
        some = slice(part * heads // 2, (part + 1) * heads // 2)
        total = mm(jnp.concatenate(own[some], axis=0), grad)
        total += mm(jnp.concatenate(sibling[some], axis=0), sibling_grad)
        for n, head in enumerate(range(heads)[some]):
            for place in range(dp_count):
                at = n * side + place * size
                out_ref[place, head] = total[at : at + size].astype(bf16)


def output_kernel(attn_ref, w_ref, out_ref):
    parts = [
        jnp.concatenate(
            [attn_ref[2 * pair + side, :HDIM, :] for side in range(2)], axis=0
        ).T
        for pair in range(attn_ref.shape[0] // 2)
    ]
    out_ref[...] = mm(jnp.concatenate(parts, axis=1), w_ref[...]).astype(bf16)


def split_kernel(grads_ref, dq_ref, dk_ref, dv_ref):
    for pair in range(grads_ref.shape[0] // 2):
        cols = slice(pair * 128, pair * 128 + 128)
        for place, target in enumerate((dq_ref, dk_ref, dv_ref)):
            rows = slice(place * HDIM, place * HDIM + HDIM)
            both = [grads_ref[2 * pair + side, rows, :] for side in range(2)]
            target[:, cols] = jnp.concatenate(both, axis=0).T


def per_device(queries, keys, values, w_out, d_out, lengths):
    rows, width = queries.shape[1:]
    group = ("pair", "core")
    blocks = lax.axis_size(group)
    heads = width // HDIM
    edges = MAXDOC // rows
    half = lax.axis_index("half")
    half_scalar = half.reshape(1).astype(jnp.int32)
    side = HDIM // CORES
    dp_count = lax.axis_size("dp")
    core_scalar = lax.axis_index("core").reshape(1).astype(jnp.int32)
    total = blocks * rows + MAXDOC
    most = MAXDOC * 2 + rows + CHUNK
    shape = jax.ShapeDtypeStruct
    lists = (pltpu.SMEM((blocks,), jnp.int32), pltpu.SMEM((8,), jnp.int32))
    swap = [(0, 1), (1, 0)]

    qkv, begins, ends = call(
        prep_kernel,
        "prep",
        (shape((heads, 3 * HDIM, rows), bf16),) + (shape((blocks, rows), jnp.int32),) * 2,
        vmem(3) + smem(2),
        args=(queries[0], keys[0], values[0], lengths[0], half_scalar),
    )
    lows, highs = begins[:, 0], ends[:, rows - 1]
    d_attn = call(
        project_kernel,
        "project",
        shape((heads, HDIM, rows), bf16),
        vmem(2),
        flops=2 * rows * width * width,
        touched=2 * width * width,
        args=(d_out[0], w_out),
    )
    sibling_grad = lax.ppermute(d_out[0], "core", swap)
    qkv = lax.all_to_all(qkv, group, 0, 0, tiled=True)
    qkv, d_attn = lax.optimization_barrier((qkv, d_attn))
    near = lax.dynamic_slice_in_dim(qkv, (1 - half) * (blocks - edges), edges, 0)[:, HDIM:]
    halo = lax.ppermute(near, "half", swap)
    d_attn = lax.all_to_all(d_attn, group, 0, 0, tiled=True)

    attn, stats, kv_n, k_t = call(
        forward_kernel,
        "forward",
        (
            shape((blocks, HDIM + side, rows), bf16),
            shape((blocks, rows), f32),
            shape((total, 2 * HDIM), bf16),
            shape((HDIM, total), bf16),
        ),
        smem(3) + vmem(4),
        (pltpu.VMEM((HDIM, total), bf16), pltpu.VMEM((TOGETHER, most, rows), f32)) + lists,
        flops=10**10,
        touched=10**7,
        args=(half_scalar, lows, highs, begins, ends, qkv, halo),
    )
    upper = pl.BlockSpec((blocks, HDIM, rows), lambda step: (0, 0, 0))
    grads, edge, dhalo = call(
        backward_kernel,
        "backward",
        (
            shape((blocks, 3 * HDIM, rows), bf16),
            shape((edges, 2 * HDIM, rows), f32),
            shape((edges, 2 * HDIM, rows), bf16),
        ),
        smem(3) + vmem(2) + [upper] + vmem(1) + [upper] + vmem(3),
        (pltpu.VMEM((2 * HDIM, total), f32),) + lists,
        flops=10**10,
        touched=10**7,
        grid=(1,),
        args=(half_scalar, lows, highs, begins, ends, qkv, d_attn, attn, stats, kv_n, k_t),
    )
    attn = lax.all_to_all(attn, group, 0, 0, tiled=True)
    dhalo = lax.ppermute(dhalo, "half", swap)
    attn, grads, edge = lax.optimization_barrier((attn, grads, edge))
    chip_sum = call(
        weight_kernel,
        "weight",
        shape((dp_count, heads, side // dp_count, width), bf16),
        smem(1) + vmem(3),
        flops=2 * rows * width * width,
        touched=4 * width * width,
        args=(core_scalar, attn, d_out[0], sibling_grad),
    )
    dhalo, chip_sum = lax.optimization_barrier((dhalo, chip_sum))
    mine = lax.axis_index("dp")
    column = lax.dynamic_index_in_dim(chip_sum, mine, 0, keepdims=False).astype(f32)
    for step in range(1, dp_count):
        part = lax.dynamic_index_in_dim(chip_sum, (mine + step) % dp_count, 0, keepdims=False)
        moves = [(d, (d + step) % dp_count) for d in range(dp_count)]
        column = column + lax.ppermute(part, "dp", moves).astype(f32)

    edge = (edge + dhalo.astype(f32)).astype(bf16)
    grads = lax.dynamic_update_slice(grads, edge, ((1 - half) * (blocks - edges), HDIM, 0))
    grads = lax.all_to_all(grads, group, 0, 0, tiled=True)
    column, grads = lax.optimization_barrier((column.astype(bf16), grads))
    parts = lax.all_to_all(column, ("half", "pair"), 0, 0, tiled=True)
    w_grad = jnp.sum(parts.astype(f32), axis=0)

    flat = shape((rows, width), bf16)
    output = call(
        output_kernel,
        "output",
        flat,
        vmem(2),
        flops=2 * rows * width * width,
        touched=2 * width * width,
        args=(attn, w_out),
    )
    d_queries, d_keys, d_values = call(
        split_kernel, "split", (flat,) * 3, vmem(1), args=(grads,)
    )
    return (output[None], d_queries[None], d_keys[None], d_values[None], w_grad)


def solution(mesh):
    ctx_count, dp_count = mesh.devices.shape
    pairs = ctx_count // (HALVES * CORES)
    fine = Mesh(
        mesh.devices.reshape(HALVES, pairs, CORES, dp_count), ("half", "pair", "core", "dp")
    )
    ctx = ("half", "pair", "core")
    tokens = P("dp", ctx, None)
    return jax.shard_map(
        per_device,
        mesh=fine,
        in_specs=(tokens, tokens, tokens, P(), tokens, P("dp", None)),
        out_specs=(tokens, tokens, tokens, tokens, P(ctx + ("dp",), None)),
        check_vma=False,
    )
```

```python
import jax
import jax.numpy as jnp
from jax import lax
from jax.experimental import pallas as pl
from jax.experimental.pallas import tpu as pltpu
from jax.sharding import Mesh
from jax.sharding import PartitionSpec as P

HDIM = 64
HALVES = 2
CORES = 2
MAXDOC = 1024
CHUNK = 256
STEP = 128
STATIC_COUNTS = (3, 4, 5, 6, 8, 10, 12)
TOGETHER = 2
AHEAD = 2
VMEM_LIMIT = 60 * 1024 * 1024
SCALE = 0.125
LOG2E = 1.4426950408889634
EXP2_SCALE = SCALE * LOG2E
MASKED = -1e30

f32 = jnp.float32
bf16 = jnp.bfloat16


def mm(a, b):
    return jnp.dot(a, b, preferred_element_type=f32)


def mm_nt(a, b):
    return lax.dot_general(a, b, (((1,), (1,)), ((), ())), preferred_element_type=f32)


def vmem(count):
    return [pl.BlockSpec(memory_space=pltpu.VMEM)] * count


def smem(count):
    return [pl.BlockSpec(memory_space=pltpu.SMEM)] * count


def call(kernel, name, out_shape, in_specs, scratch=(), flops=0, touched=0, grid=(), *, args):
    many = isinstance(out_shape, tuple)
    return pl.pallas_call(
        kernel,
        out_shape=out_shape,
        grid=grid,
        in_specs=in_specs,
        out_specs=vmem(len(out_shape)) if many else vmem(1)[0],
        scratch_shapes=list(scratch),
        compiler_params=pltpu.CompilerParams(vmem_limit_bytes=VMEM_LIMIT),
        cost_estimate=pl.CostEstimate(flops=flops, bytes_accessed=touched, transcendentals=0),
        name=name,
    )(*args)


def prep_kernel(q_ref, k_ref, v_ref, len_ref, half_ref, qkv_ref, st_ref, en_ref):
    heads = qkv_ref.shape[0]
    own = st_ref.shape[0] * st_ref.shape[1]
    half = half_ref[0]
    for pair in range(heads // 2):
        cols = slice(pair * 128, pair * 128 + 128)
        for place, source in enumerate((q_ref, k_ref, v_ref)):
            turned = source[:, cols].T
            for side in range(2):
                qkv_ref[2 * pair + side, place * HDIM : place * HDIM + HDIM, :] = turned[
                    side * HDIM : side * HDIM + HDIM
                ]
    shape = st_ref.shape
    position = (
        lax.broadcasted_iota(jnp.int32, shape, 0) * shape[1]
        + lax.broadcasted_iota(jnp.int32, shape, 1)
        + half * own
    )

    def document(index, carry):
        end, begins, ends = carry
        end = end + len_ref[index]
        before = end <= position
        begins = jnp.where(before, end, begins)
        ends = jnp.where(before, ends, jnp.minimum(ends, end))
        return end, begins, ends

    _, begins, ends = lax.fori_loop(
        0,
        len_ref.shape[0],
        document,
        (jnp.int32(0), jnp.zeros(shape, jnp.int32), jnp.full(shape, 2 * own, jnp.int32)),
        unroll=8,
    )
    first = half * (own - MAXDOC)
    st_ref[...] = begins - first
    en_ref[...] = ends - first


def project_kernel(g_ref, w_ref, da_ref):
    grad = g_ref[...]
    for four in range(da_ref.shape[0] // 4):
        part = mm_nt(w_ref[four * 256 : four * 256 + 256, :], grad).astype(bf16)
        for n in range(4):
            da_ref[4 * four + n] = part[n * HDIM : n * HDIM + HDIM]


def span(lo_ref, hi_ref, index):
    low = (lo_ref[index] // STEP) * STEP
    return low, (hi_ref[index] - low + STEP - 1) // STEP


def by_count(lo_ref, hi_ref, total, order, tally, run):
    blocks = lo_ref.shape[0]
    kinds = len(STATIC_COUNTS) + 1

    def kind_of(index):
        count = span(lo_ref, hi_ref, index)[1]
        return sum([(count > fixed).astype(jnp.int32) for fixed in STATIC_COUNTS])

    for kind in range(kinds):
        tally[kind] = 0

    @pl.loop(0, blocks)
    def _(index):
        kind = kind_of(index)
        tally[kind] = tally[kind] + 1

    ends, end = [], 0
    for kind in range(kinds):
        begin, end = end, end + tally[kind]
        tally[kind] = begin
        ends.append(end)

    @pl.loop(0, blocks)
    def _(index):
        kind = kind_of(index)
        place = tally[kind]
        tally[kind] = place + 1
        order[place] = index

    begin = 0
    for kind, end in enumerate(ends):

        @pl.loop(begin // TOGETHER, end // TOGETHER)
        def _(place, kind=kind):
            members = [order[place * TOGETHER + n] for n in range(TOGETHER)]
            spans = [span(lo_ref, hi_ref, index) for index in members]
            if kind < kinds - 1:
                size = STATIC_COUNTS[kind] * STEP
                chunks = [(at, min(CHUNK, size - at)) for at in range(0, size, CHUNK)]
            else:
                count = spans[0][1]
                for _, more in spans[1:]:
                    count = jnp.maximum(count, more)
                chunks = (count * STEP + CHUNK - 1) // CHUNK
                size = chunks * CHUNK
            run(members, [jnp.minimum(low, total - size) for low, _ in spans], chunks)

        begin = end


def over(chunks, body, carry):
    if isinstance(chunks, list):
        for chunk in chunks:
            carry = body(chunk, carry)
        return carry
    return lax.fori_loop(
        0, chunks, lambda n, c: body((pl.multiple_of(n * CHUNK, CHUNK), CHUNK), c), carry
    )


def forward_kernel(
    half_ref, lo_ref, hi_ref, st_ref, en_ref, qkv_ref, halo_ref,
    attn_ref, stat_ref, kv_n, k_t, v_t, probs, order, tally,
):
    blocks, _, rows = qkv_ref.shape
    edges = halo_ref.shape[0]
    half = half_ref[0]
    total = kv_n.shape[0]

    def place(block, at):
        at = pl.multiple_of(at, rows)
        k_t[:, pl.ds(at, rows)] = block[:HDIM]
        v_t[:, pl.ds(at, rows)] = block[HDIM:]
        kv_n[pl.ds(at, rows), :] = block.T

    for index in range(blocks):
        place(qkv_ref[index, HDIM:, :], half * MAXDOC + index * rows)
    for index in range(edges):
        place(halo_ref[index], (1 - half) * blocks * rows + index * rows)

    offset = lax.broadcasted_iota(jnp.int32, (CHUNK, rows), 0)

    def run(members, lows, chunks):
        many = range(len(members))
        queries, begins, lengths = [], [], []
        for index in members:
            query = qkv_ref[index, :HDIM, :]
            queries.append(jnp.concatenate([query, jnp.zeros_like(query)], axis=0))
            begins.append(st_ref[pl.ds(index, 1), :])
            lengths.append((en_ref[pl.ds(index, 1), :] - begins[-1]).astype(jnp.uint32))

        def score(chunk, tops):
            start, size = chunk
            news = []
            for n in many:
                base = pl.multiple_of(lows[n] + start, STEP)
                scores = mm(kv_n[pl.ds(base, size), :], queries[n])
                inside = (offset[:size] - (begins[n] - base)).astype(jnp.uint32) < lengths[n]
                scores = jnp.where(inside, scores, MASKED)
                probs[n, pl.ds(start, size), :] = scores
                most = jnp.max(scores.reshape(size // 8, 8, rows), axis=0)
                news.append(jnp.maximum(tops[n], most))
            return news

        tops = over(chunks, score, [jnp.full((8, rows), MASKED, f32)] * len(members))
        tops = [jnp.max(top, axis=0, keepdims=True) for top in tops]

        def weigh(chunk, carry):
            start, size = chunk
            news = []
            for n in many:
                sums, out = carry[n]
                keys = pl.ds(pl.multiple_of(lows[n] + start, STEP), size)
                weights = jnp.exp2((probs[n, pl.ds(start, size), :] - tops[n]) * EXP2_SCALE)
                sums = sums + jnp.sum(weights.reshape(size // 8, 8, rows), axis=0)
                news.append((sums, out + mm(v_t[:, keys], weights.astype(bf16))))
            return news

        nothing = (jnp.zeros((8, rows), f32), jnp.zeros((HDIM, rows), f32))
        totals = over(chunks, weigh, [nothing] * len(members))
        for index, top, (sums, out) in zip(members, tops, totals):
            sums = jnp.sum(sums, axis=0, keepdims=True)
            attn = (out * (1.0 / sums)).astype(bf16)
            attn_ref[index, :HDIM, :] = attn
            side = HDIM // CORES
            sibling = index + 1 - 2 * (index % CORES)
            attn_ref[sibling, HDIM:, :] = jnp.where(
                index % CORES == 0, attn[side:], attn[:side]
            )
            stat_ref[pl.ds(index, 1), :] = top * EXP2_SCALE + jnp.log(sums) * LOG2E

    by_count(lo_ref, hi_ref, total, order, tally, run)


def backward_kernel(
    half_ref, lo_ref, hi_ref, st_ref, en_ref, q_ref, da_ref, attn_ref, stat_ref, kv_n, k_t,
    grads_ref, edge_ref, dhalo_ref, acc, order, tally,
):
    blocks, _, rows = q_ref.shape
    edges = edge_ref.shape[0]
    half = half_ref[0]
    total = kv_n.shape[0]

    @pl.loop(0, total // CHUNK)
    def _(chunk):
        keys = pl.ds(pl.multiple_of(chunk * CHUNK, CHUNK), CHUNK)
        acc[:, keys] = jnp.zeros((acc.shape[0], CHUNK), f32)

    offset = lax.broadcasted_iota(jnp.int32, (CHUNK, rows), 0)

    def run(members, lows, chunks):
        fixed = []
        for index in members:
            query_t = q_ref[index]
            grad_t = da_ref[index]
            nothing = jnp.zeros_like(query_t)
            begin = st_ref[pl.ds(index, 1), :]
            attn = attn_ref[index].astype(f32)
            fixed.append(
                dict(
                    query_t=query_t,
                    grad_t=grad_t,
                    query=jnp.concatenate([query_t, nothing], axis=0),
                    grad=jnp.concatenate([nothing, grad_t], axis=0),
                    begin=begin,
                    length=(en_ref[pl.ds(index, 1), :] - begin).astype(jnp.uint32),
                    log_total=stat_ref[pl.ds(index, 1), :],
                    delta=jnp.sum(attn * grad_t.astype(f32), axis=0, keepdims=True),
                )
            )

        def products(n, chunk):
            start, size = chunk
            both = kv_n[pl.ds(pl.multiple_of(lows[n] + start, STEP), size), :]
            return mm(both, fixed[n]["query"]), mm(both, fixed[n]["grad"])

        def derive(n, chunk, scores, d_probs, d_query):
            start, size = chunk
            own = fixed[n]
            base = pl.multiple_of(lows[n] + start, STEP)
            keys = pl.ds(base, size)
            inside = (offset[:size] - (own["begin"] - base)).astype(jnp.uint32) < own["length"]
            exponent = scores * EXP2_SCALE - own["log_total"]
            likely = jnp.exp2(jnp.where(inside, exponent, MASKED))
            d_scores = (likely * (d_probs - own["delta"])).astype(bf16)
            acc[:HDIM, keys] += mm_nt(own["query_t"], d_scores)
            acc[HDIM:, keys] += mm_nt(own["grad_t"], likely.astype(bf16))
            return d_query + mm(k_t[:, keys], d_scores)

        d_queries = [jnp.zeros((HDIM, rows), f32)] * len(members)
        if isinstance(chunks, list):
            items = [(n, chunk) for chunk in chunks for n in range(len(members))]
            ahead = [products(*item) for item in items[:AHEAD]]
            for place, (n, chunk) in enumerate(items):
                now = ahead.pop(0)
                if place + AHEAD < len(items):
                    ahead.append(products(*items[place + AHEAD]))
                d_queries[n] = derive(n, chunk, *now, d_queries[n])
        else:

            def step(chunk, sums):
                return [
                    derive(n, chunk, *products(n, chunk), sums[n]) for n in range(len(members))
                ]

            d_queries = over(chunks, step, d_queries)
        for index, d_query in zip(members, d_queries):
            grads_ref[index, :HDIM, :] = (d_query * SCALE).astype(bf16)

    by_count(lo_ref, hi_ref, total, order, tally, run)

    feature = lax.broadcasted_iota(jnp.int32, (2 * HDIM, rows), 0)
    factor = jnp.where(feature < HDIM, SCALE, 1.0)
    own_at = half * MAXDOC

    @pl.loop(0, blocks)
    def _(index):
        at = pl.multiple_of(own_at + index * rows, rows)
        grads_ref[index, HDIM:, :] = (acc[:, pl.ds(at, rows)] * factor).astype(bf16)

    @pl.loop(0, edges)
    def _(index):
        at = pl.multiple_of((1 - half) * blocks * rows + index * rows, rows)
        dhalo_ref[index] = (acc[:, pl.ds(at, rows)] * factor).astype(bf16)
        at = pl.multiple_of(own_at + (1 - half) * (blocks - edges) * rows + index * rows, rows)
        edge_ref[index] = acc[:, pl.ds(at, rows)] * factor


def weight_kernel(core_ref, attn_ref, g_ref, sibling_ref, out_ref):
    grad, sibling_grad = g_ref[...], sibling_ref[...]
    mine = core_ref[0] == 0
    side = HDIM // CORES
    dp_count, heads = out_ref.shape[:2]
    size = side // dp_count
    own, sibling = [], []
    for head in range(heads):
        rows = attn_ref[head, :HDIM, :]
        own.append(jnp.where(mine, rows[:side], rows[side:]))
        sibling.append(attn_ref[head, HDIM:, :])
    for part in range(2):
        some = slice(part * heads // 2, (part + 1) * heads // 2)
        total = mm(jnp.concatenate(own[some], axis=0), grad)
        total += mm(jnp.concatenate(sibling[some], axis=0), sibling_grad)
        for n, head in enumerate(range(heads)[some]):
            for place in range(dp_count):
                at = n * side + place * size
                out_ref[place, head] = total[at : at + size].astype(bf16)


def output_kernel(attn_ref, w_ref, out_ref):
    parts = [
        jnp.concatenate(
            [attn_ref[2 * pair + side, :HDIM, :] for side in range(2)], axis=0
        ).T
        for pair in range(attn_ref.shape[0] // 2)
    ]
    out_ref[...] = mm(jnp.concatenate(parts, axis=1), w_ref[...]).astype(bf16)


def split_kernel(grads_ref, dq_ref, dk_ref, dv_ref):
    for pair in range(grads_ref.shape[0] // 2):
        cols = slice(pair * 128, pair * 128 + 128)
        for place, target in enumerate((dq_ref, dk_ref, dv_ref)):
            rows = slice(place * HDIM, place * HDIM + HDIM)
            both = [grads_ref[2 * pair + side, rows, :] for side in range(2)]
            target[:, cols] = jnp.concatenate(both, axis=0).T


def per_device(queries, keys, values, w_out, d_out, lengths):
    rows, width = queries.shape[1:]
    group = ("pair", "core")
    blocks = lax.axis_size(group)
    heads = width // HDIM
    edges = MAXDOC // rows
    half = lax.axis_index("half")
    half_scalar = half.reshape(1).astype(jnp.int32)
    side = HDIM // CORES
    dp_count = lax.axis_size("dp")
    core_scalar = lax.axis_index("core").reshape(1).astype(jnp.int32)
    total = blocks * rows + MAXDOC
    most = MAXDOC * 2 + rows + CHUNK
    shape = jax.ShapeDtypeStruct
    lists = (pltpu.SMEM((blocks,), jnp.int32), pltpu.SMEM((8,), jnp.int32))
    swap = [(0, 1), (1, 0)]

    qkv, begins, ends = call(
        prep_kernel,
        "prep",
        (shape((heads, 3 * HDIM, rows), bf16),) + (shape((blocks, rows), jnp.int32),) * 2,
        vmem(3) + smem(2),
        args=(queries[0], keys[0], values[0], lengths[0], half_scalar),
    )
    lows, highs = begins[:, 0], ends[:, rows - 1]
    d_attn = call(
        project_kernel,
        "project",
        shape((heads, HDIM, rows), bf16),
        vmem(2),
        flops=2 * rows * width * width,
        touched=2 * width * width,
        args=(d_out[0], w_out),
    )
    sibling_grad = lax.ppermute(d_out[0], "core", swap)
    qkv = lax.all_to_all(qkv, group, 0, 0, tiled=True)
    qkv, d_attn = lax.optimization_barrier((qkv, d_attn))
    near = lax.dynamic_slice_in_dim(qkv, (1 - half) * (blocks - edges), edges, 0)[:, HDIM:]
    halo = lax.ppermute(near, "half", swap)
    d_attn = lax.all_to_all(d_attn, group, 0, 0, tiled=True)

    attn, stats, kv_n, k_t = call(
        forward_kernel,
        "forward",
        (
            shape((blocks, HDIM + side, rows), bf16),
            shape((blocks, rows), f32),
            shape((total, 2 * HDIM), bf16),
            shape((HDIM, total), bf16),
        ),
        smem(3) + vmem(4),
        (pltpu.VMEM((HDIM, total), bf16), pltpu.VMEM((TOGETHER, most, rows), f32)) + lists,
        flops=10**10,
        touched=10**7,
        args=(half_scalar, lows, highs, begins, ends, qkv, halo),
    )
    upper = pl.BlockSpec((blocks, HDIM, rows), lambda step: (0, 0, 0))
    grads, edge, dhalo = call(
        backward_kernel,
        "backward",
        (
            shape((blocks, 3 * HDIM, rows), bf16),
            shape((edges, 2 * HDIM, rows), f32),
            shape((edges, 2 * HDIM, rows), bf16),
        ),
        smem(3) + vmem(2) + [upper] + vmem(1) + [upper] + vmem(3),
        (pltpu.VMEM((2 * HDIM, total), f32),) + lists,
        flops=10**10,
        touched=10**7,
        grid=(1,),
        args=(half_scalar, lows, highs, begins, ends, qkv, d_attn, attn, stats, kv_n, k_t),
    )
    attn = lax.all_to_all(attn, group, 0, 0, tiled=True)
    dhalo = lax.ppermute(dhalo, "half", swap)
    attn, grads, edge = lax.optimization_barrier((attn, grads, edge))
    chip_sum = call(
        weight_kernel,
        "weight",
        shape((dp_count, heads, side // dp_count, width), bf16),
        smem(1) + vmem(3),
        flops=2 * rows * width * width,
        touched=4 * width * width,
        args=(core_scalar, attn, d_out[0], sibling_grad),
    )
    dhalo, chip_sum = lax.optimization_barrier((dhalo, chip_sum))
    mine = lax.axis_index("dp")
    column = lax.dynamic_index_in_dim(chip_sum, mine, 0, keepdims=False).astype(f32)
    for step in range(1, dp_count):
        part = lax.dynamic_index_in_dim(chip_sum, (mine + step) % dp_count, 0, keepdims=False)
        moves = [(d, (d + step) % dp_count) for d in range(dp_count)]
        column = column + lax.ppermute(part, "dp", moves).astype(f32)

    edge = (edge + dhalo.astype(f32)).astype(bf16)
    grads = lax.dynamic_update_slice(grads, edge, ((1 - half) * (blocks - edges), HDIM, 0))
    grads = lax.all_to_all(grads, group, 0, 0, tiled=True)
    column, grads = lax.optimization_barrier((column.astype(bf16), grads))
    parts = lax.all_to_all(column, ("half", "pair"), 0, 0, tiled=True)
    w_grad = jnp.sum(parts.astype(f32), axis=0)

    flat = shape((rows, width), bf16)
    output = call(
        output_kernel,
        "output",
        flat,
        vmem(2),
        flops=2 * rows * width * width,
        touched=2 * width * width,
        args=(attn, w_out),
    )
    d_queries, d_keys, d_values = call(
        split_kernel, "split", (flat,) * 3, vmem(1), args=(grads,)
    )
    return (output[None], d_queries[None], d_keys[None], d_values[None], w_grad)


def solution(mesh):
    ctx_count, dp_count = mesh.devices.shape
    pairs = ctx_count // (HALVES * CORES)
    fine = Mesh(
        mesh.devices.reshape(HALVES, pairs, CORES, dp_count), ("half", "pair", "core", "dp")
    )
    ctx = ("half", "pair", "core")
    tokens = P("dp", ctx, None)
    return jax.shard_map(
        per_device,
        mesh=fine,
        in_specs=(tokens, tokens, tokens, P(), tokens, P("dp", None)),
        out_specs=(tokens, tokens, tokens, tokens, P(ctx + ("dp",), None)),
        check_vma=False,
    )
```

```python
import jax
import jax.numpy as jnp
from jax import lax
from jax.experimental import pallas as pl
from jax.experimental.pallas import tpu as pltpu
from jax.sharding import Mesh
from jax.sharding import PartitionSpec as P

HDIM = 64
HALVES = 2
CORES = 2
MAXDOC = 1024
CHUNK = 256
STEP = 128
STATIC_COUNTS = (2, 3, 4, 5, 6)
TOGETHER = 2
AHEAD = 2
VMEM_LIMIT = 60 * 1024 * 1024
SCALE = 0.125
LOG2E = 1.4426950408889634
EXP2_SCALE = SCALE * LOG2E
MASKED = -1e30

f32 = jnp.float32
bf16 = jnp.bfloat16


def mm(a, b):
    return jnp.dot(a, b, preferred_element_type=f32)


def mm_nt(a, b):
    return lax.dot_general(a, b, (((1,), (1,)), ((), ())), preferred_element_type=f32)


def vmem(count):
    return [pl.BlockSpec(memory_space=pltpu.VMEM)] * count


def smem(count):
    return [pl.BlockSpec(memory_space=pltpu.SMEM)] * count


def call(kernel, name, out_shape, in_specs, scratch=(), flops=0, touched=0, grid=(), *, args):
    many = isinstance(out_shape, tuple)
    return pl.pallas_call(
        kernel,
        out_shape=out_shape,
        grid=grid,
        in_specs=in_specs,
        out_specs=vmem(len(out_shape)) if many else vmem(1)[0],
        scratch_shapes=list(scratch),
        compiler_params=pltpu.CompilerParams(vmem_limit_bytes=VMEM_LIMIT),
        cost_estimate=pl.CostEstimate(flops=flops, bytes_accessed=touched, transcendentals=0),
        name=name,
    )(*args)


def prep_kernel(q_ref, k_ref, v_ref, len_ref, half_ref, qkv_ref, st_ref, en_ref):
    heads = qkv_ref.shape[0]
    own = st_ref.shape[0] * st_ref.shape[1]
    half = half_ref[0]
    for pair in range(heads // 2):
        cols = slice(pair * 128, pair * 128 + 128)
        for place, source in enumerate((q_ref, k_ref, v_ref)):
            turned = source[:, cols].T
            for side in range(2):
                qkv_ref[2 * pair + side, place * HDIM : place * HDIM + HDIM, :] = turned[
                    side * HDIM : side * HDIM + HDIM
                ]
    shape = st_ref.shape
    position = (
        lax.broadcasted_iota(jnp.int32, shape, 0) * shape[1]
        + lax.broadcasted_iota(jnp.int32, shape, 1)
        + half * own
    )

    def document(index, carry):
        end, begins, ends = carry
        end = end + len_ref[index]
        before = end <= position
        begins = jnp.where(before, end, begins)
        ends = jnp.where(before, ends, jnp.minimum(ends, end))
        return end, begins, ends

    _, begins, ends = lax.fori_loop(
        0,
        len_ref.shape[0],
        document,
        (jnp.int32(0), jnp.zeros(shape, jnp.int32), jnp.full(shape, 2 * own, jnp.int32)),
        unroll=8,
    )
    first = half * (own - MAXDOC)
    st_ref[...] = begins - first
    en_ref[...] = ends - first


def project_kernel(g_ref, w_ref, da_ref):
    grad = g_ref[...]
    for four in range(da_ref.shape[0] // 4):
        part = mm_nt(w_ref[four * 256 : four * 256 + 256, :], grad).astype(bf16)
        for n in range(4):
            da_ref[4 * four + n] = part[n * HDIM : n * HDIM + HDIM]


def span(lo_ref, hi_ref, index):
    low = (lo_ref[index] // STEP) * STEP
    return low, (hi_ref[index] - low + CHUNK - 1) // CHUNK


def by_count(lo_ref, hi_ref, total, order, tally, run):
    blocks = lo_ref.shape[0]
    least, kinds = STATIC_COUNTS[0], len(STATIC_COUNTS) + 1

    def kind_of(index):
        return jnp.clip(span(lo_ref, hi_ref, index)[1] - least, 0, kinds - 1)

    for kind in range(kinds):
        tally[kind] = 0

    @pl.loop(0, blocks)
    def _(index):
        kind = kind_of(index)
        tally[kind] = tally[kind] + 1

    ends, end = [], 0
    for kind in range(kinds):
        begin, end = end, end + tally[kind]
        tally[kind] = begin
        ends.append(end)

    @pl.loop(0, blocks)
    def _(index):
        kind = kind_of(index)
        place = tally[kind]
        tally[kind] = place + 1
        order[place] = index

    begin = 0
    for kind, end in enumerate(ends):

        @pl.loop(begin // TOGETHER, end // TOGETHER)
        def _(place, kind=kind):
            members = [order[place * TOGETHER + n] for n in range(TOGETHER)]
            spans = [span(lo_ref, hi_ref, index) for index in members]
            if kind < kinds - 1:
                count = STATIC_COUNTS[kind]
            else:
                count = spans[0][1]
                for _, other in spans[1:]:
                    count = jnp.maximum(count, other)
            lows = [jnp.minimum(low, total - count * CHUNK) for low, _ in spans]
            run(members, lows, count)

        begin = end


def over(count, body, carry):
    if isinstance(count, int):
        for chunk in range(count):
            carry = body(chunk * CHUNK, carry)
        return carry
    return lax.fori_loop(
        0, count, lambda chunk, c: body(pl.multiple_of(chunk * CHUNK, CHUNK), c), carry
    )


def forward_kernel(
    half_ref, lo_ref, hi_ref, st_ref, en_ref, qkv_ref, halo_ref,
    attn_ref, stat_ref, kv_n, k_t, v_t, probs, order, tally,
):
    blocks, _, rows = qkv_ref.shape
    edges = halo_ref.shape[0]
    half = half_ref[0]
    total = kv_n.shape[0]

    def place(block, at):
        at = pl.multiple_of(at, rows)
        k_t[:, pl.ds(at, rows)] = block[:HDIM]
        v_t[:, pl.ds(at, rows)] = block[HDIM:]
        kv_n[pl.ds(at, rows), :] = block.T

    for index in range(blocks):
        place(qkv_ref[index, HDIM:, :], half * MAXDOC + index * rows)
    for index in range(edges):
        place(halo_ref[index], (1 - half) * blocks * rows + index * rows)

    offset = lax.broadcasted_iota(jnp.int32, (CHUNK, rows), 0)

    def run(members, lows, count):
        many = range(len(members))
        queries, begins, lengths = [], [], []
        for index in members:
            query = qkv_ref[index, :HDIM, :]
            queries.append(jnp.concatenate([query, jnp.zeros_like(query)], axis=0))
            begins.append(st_ref[pl.ds(index, 1), :])
            lengths.append((en_ref[pl.ds(index, 1), :] - begins[-1]).astype(jnp.uint32))

        def score(start, tops):
            news = []
            for n in many:
                base = pl.multiple_of(lows[n] + start, STEP)
                scores = mm(kv_n[pl.ds(base, CHUNK), :], queries[n])
                inside = (offset - (begins[n] - base)).astype(jnp.uint32) < lengths[n]
                scores = jnp.where(inside, scores, MASKED)
                probs[n, pl.ds(start, CHUNK), :] = scores
                most = jnp.max(scores.reshape(CHUNK // 8, 8, rows), axis=0)
                news.append(jnp.maximum(tops[n], most))
            return news

        tops = over(count, score, [jnp.full((8, rows), MASKED, f32)] * len(members))
        tops = [jnp.max(top, axis=0, keepdims=True) for top in tops]

        def weigh(start, carry):
            news = []
            for n in many:
                sums, out = carry[n]
                keys = pl.ds(pl.multiple_of(lows[n] + start, STEP), CHUNK)
                weights = jnp.exp2((probs[n, pl.ds(start, CHUNK), :] - tops[n]) * EXP2_SCALE)
                sums = sums + jnp.sum(weights.reshape(CHUNK // 8, 8, rows), axis=0)
                news.append((sums, out + mm(v_t[:, keys], weights.astype(bf16))))
            return news

        nothing = (jnp.zeros((8, rows), f32), jnp.zeros((HDIM, rows), f32))
        totals = over(count, weigh, [nothing] * len(members))
        for index, top, (sums, out) in zip(members, tops, totals):
            sums = jnp.sum(sums, axis=0, keepdims=True)
            attn = (out * (1.0 / sums)).astype(bf16)
            attn_ref[index, :HDIM, :] = attn
            side = HDIM // CORES
            sibling = index + 1 - 2 * (index % CORES)
            attn_ref[sibling, HDIM:, :] = jnp.where(
                index % CORES == 0, attn[side:], attn[:side]
            )
            stat_ref[pl.ds(index, 1), :] = top * EXP2_SCALE + jnp.log(sums) * LOG2E

    by_count(lo_ref, hi_ref, total, order, tally, run)


def backward_kernel(
    half_ref, lo_ref, hi_ref, st_ref, en_ref, q_ref, da_ref, attn_ref, stat_ref, kv_n, k_t,
    grads_ref, edge_ref, dhalo_ref, acc, order, tally,
):
    blocks, _, rows = q_ref.shape
    edges = edge_ref.shape[0]
    half = half_ref[0]
    total = kv_n.shape[0]

    @pl.loop(0, total // CHUNK, unroll=4)
    def _(chunk):
        keys = pl.ds(pl.multiple_of(chunk * CHUNK, CHUNK), CHUNK)
        acc[:, keys] = jnp.zeros((acc.shape[0], CHUNK), f32)

    offset = lax.broadcasted_iota(jnp.int32, (CHUNK, rows), 0)

    def run(members, lows, count):
        fixed = []
        for index in members:
            query_t = q_ref[index]
            grad_t = da_ref[index]
            nothing = jnp.zeros_like(query_t)
            begin = st_ref[pl.ds(index, 1), :]
            attn = attn_ref[index].astype(f32)
            fixed.append(
                dict(
                    query_t=query_t,
                    grad_t=grad_t,
                    query=jnp.concatenate([query_t, nothing], axis=0),
                    grad=jnp.concatenate([nothing, grad_t], axis=0),
                    begin=begin,
                    length=(en_ref[pl.ds(index, 1), :] - begin).astype(jnp.uint32),
                    log_total=stat_ref[pl.ds(index, 1), :],
                    delta=jnp.sum(attn * grad_t.astype(f32), axis=0, keepdims=True),
                )
            )

        def products(n, start):
            both = kv_n[pl.ds(pl.multiple_of(lows[n] + start, STEP), CHUNK), :]
            return mm(both, fixed[n]["query"]), mm(both, fixed[n]["grad"])

        def derive(n, start, scores, d_probs, d_query):
            own = fixed[n]
            base = pl.multiple_of(lows[n] + start, STEP)
            keys = pl.ds(base, CHUNK)
            inside = (offset - (own["begin"] - base)).astype(jnp.uint32) < own["length"]
            exponent = scores * EXP2_SCALE - own["log_total"]
            likely = jnp.exp2(jnp.where(inside, exponent, MASKED))
            d_scores = (likely * (d_probs - own["delta"])).astype(bf16)
            acc[:HDIM, keys] += mm_nt(own["query_t"], d_scores)
            acc[HDIM:, keys] += mm_nt(own["grad_t"], likely.astype(bf16))
            return d_query + mm(k_t[:, keys], d_scores)

        d_queries = [jnp.zeros((HDIM, rows), f32)] * len(members)
        if isinstance(count, int):
            items = [(n, c * CHUNK) for c in range(count) for n in range(len(members))]
            ahead = [products(*item) for item in items[:AHEAD]]
            for place, (n, start) in enumerate(items):
                now = ahead.pop(0)
                if place + AHEAD < len(items):
                    ahead.append(products(*items[place + AHEAD]))
                d_queries[n] = derive(n, start, *now, d_queries[n])
        else:

            def step(start, sums):
                return [
                    derive(n, start, *products(n, start), sums[n]) for n in range(len(members))
                ]

            d_queries = over(count, step, d_queries)
        for index, d_query in zip(members, d_queries):
            grads_ref[index, :HDIM, :] = (d_query * SCALE).astype(bf16)

    by_count(lo_ref, hi_ref, total, order, tally, run)

    feature = lax.broadcasted_iota(jnp.int32, (2 * HDIM, rows), 0)
    factor = jnp.where(feature < HDIM, SCALE, 1.0)
    own_at = half * MAXDOC

    @pl.loop(0, blocks, unroll=4)
    def _(index):
        at = pl.multiple_of(own_at + index * rows, rows)
        grads_ref[index, HDIM:, :] = (acc[:, pl.ds(at, rows)] * factor).astype(bf16)

    @pl.loop(0, edges, unroll=4)
    def _(index):
        at = pl.multiple_of((1 - half) * blocks * rows + index * rows, rows)
        dhalo_ref[index] = (acc[:, pl.ds(at, rows)] * factor).astype(bf16)
        at = pl.multiple_of(own_at + (1 - half) * (blocks - edges) * rows + index * rows, rows)
        edge_ref[index] = acc[:, pl.ds(at, rows)] * factor


def weight_kernel(core_ref, attn_ref, g_ref, sibling_ref, out_ref):
    grad, sibling_grad = g_ref[...], sibling_ref[...]
    mine = core_ref[0] == 0
    side = HDIM // CORES
    dp_count, heads = out_ref.shape[:2]
    size = side // dp_count
    own, sibling = [], []
    for head in range(heads):
        rows = attn_ref[head, :HDIM, :]
        own.append(jnp.where(mine, rows[:side], rows[side:]))
        sibling.append(attn_ref[head, HDIM:, :])
    for part in range(2):
        some = slice(part * heads // 2, (part + 1) * heads // 2)
        total = mm(jnp.concatenate(own[some], axis=0), grad)
        total += mm(jnp.concatenate(sibling[some], axis=0), sibling_grad)
        for n, head in enumerate(range(heads)[some]):
            for place in range(dp_count):
                at = n * side + place * size
                out_ref[place, head] = total[at : at + size].astype(bf16)


def output_kernel(attn_ref, w_ref, out_ref):
    parts = [
        jnp.concatenate(
            [attn_ref[2 * pair + side, :HDIM, :] for side in range(2)], axis=0
        ).T
        for pair in range(attn_ref.shape[0] // 2)
    ]
    out_ref[...] = mm(jnp.concatenate(parts, axis=1), w_ref[...]).astype(bf16)


def split_kernel(grads_ref, dq_ref, dk_ref, dv_ref):
    for pair in range(grads_ref.shape[0] // 2):
        cols = slice(pair * 128, pair * 128 + 128)
        for place, target in enumerate((dq_ref, dk_ref, dv_ref)):
            rows = slice(place * HDIM, place * HDIM + HDIM)
            both = [grads_ref[2 * pair + side, rows, :] for side in range(2)]
            target[:, cols] = jnp.concatenate(both, axis=0).T


def per_device(queries, keys, values, w_out, d_out, lengths):
    rows, width = queries.shape[1:]
    group = ("pair", "core")
    blocks = lax.axis_size(group)
    heads = width // HDIM
    edges = MAXDOC // rows
    half = lax.axis_index("half")
    half_scalar = half.reshape(1).astype(jnp.int32)
    side = HDIM // CORES
    dp_count = lax.axis_size("dp")
    core_scalar = lax.axis_index("core").reshape(1).astype(jnp.int32)
    total = blocks * rows + MAXDOC
    most = MAXDOC * 2 + rows + CHUNK
    shape = jax.ShapeDtypeStruct
    lists = (pltpu.SMEM((blocks,), jnp.int32), pltpu.SMEM((8,), jnp.int32))
    swap = [(0, 1), (1, 0)]

    qkv, begins, ends = call(
        prep_kernel,
        "prep",
        (shape((heads, 3 * HDIM, rows), bf16),) + (shape((blocks, rows), jnp.int32),) * 2,
        vmem(3) + smem(2),
        args=(queries[0], keys[0], values[0], lengths[0], half_scalar),
    )
    lows, highs = begins[:, 0], ends[:, rows - 1]
    d_attn = call(
        project_kernel,
        "project",
        shape((heads, HDIM, rows), bf16),
        vmem(2),
        flops=2 * rows * width * width,
        touched=2 * width * width,
        args=(d_out[0], w_out),
    )
    sibling_grad = lax.ppermute(d_out[0], "core", swap)
    qkv = lax.all_to_all(qkv, group, 0, 0, tiled=True)
    qkv, d_attn = lax.optimization_barrier((qkv, d_attn))
    near = lax.dynamic_slice_in_dim(qkv, (1 - half) * (blocks - edges), edges, 0)[:, HDIM:]
    halo = lax.ppermute(near, "half", swap)
    d_attn = lax.all_to_all(d_attn, group, 0, 0, tiled=True)

    attn, stats, kv_n, k_t = call(
        forward_kernel,
        "forward",
        (
            shape((blocks, HDIM + side, rows), bf16),
            shape((blocks, rows), f32),
            shape((total, 2 * HDIM), bf16),
            shape((HDIM, total), bf16),
        ),
        smem(3) + vmem(4),
        (pltpu.VMEM((HDIM, total), bf16), pltpu.VMEM((TOGETHER, most, rows), f32)) + lists,
        flops=10**10,
        touched=10**7,
        args=(half_scalar, lows, highs, begins, ends, qkv, halo),
    )
    upper = pl.BlockSpec((blocks, HDIM, rows), lambda step: (0, 0, 0))
    grads, edge, dhalo = call(
        backward_kernel,
        "backward",
        (
            shape((blocks, 3 * HDIM, rows), bf16),
            shape((edges, 2 * HDIM, rows), f32),
            shape((edges, 2 * HDIM, rows), bf16),
        ),
        smem(3) + vmem(2) + [upper] + vmem(1) + [upper] + vmem(3),
        (pltpu.VMEM((2 * HDIM, total), f32),) + lists,
        flops=10**10,
        touched=10**7,
        grid=(1,),
        args=(half_scalar, lows, highs, begins, ends, qkv, d_attn, attn, stats, kv_n, k_t),
    )
    attn = lax.all_to_all(attn, group, 0, 0, tiled=True)
    dhalo = lax.ppermute(dhalo, "half", swap)
    attn, grads, edge = lax.optimization_barrier((attn, grads, edge))
    chip_sum = call(
        weight_kernel,
        "weight",
        shape((dp_count, heads, side // dp_count, width), bf16),
        smem(1) + vmem(3),
        flops=2 * rows * width * width,
        touched=4 * width * width,
        args=(core_scalar, attn, d_out[0], sibling_grad),
    )
    dhalo, chip_sum = lax.optimization_barrier((dhalo, chip_sum))
    mine = lax.axis_index("dp")
    column = lax.dynamic_index_in_dim(chip_sum, mine, 0, keepdims=False).astype(f32)
    for step in range(1, dp_count):
        part = lax.dynamic_index_in_dim(chip_sum, (mine + step) % dp_count, 0, keepdims=False)
        moves = [(d, (d + step) % dp_count) for d in range(dp_count)]
        column = column + lax.ppermute(part, "dp", moves).astype(f32)

    edge = (edge + dhalo.astype(f32)).astype(bf16)
    grads = lax.dynamic_update_slice(grads, edge, ((1 - half) * (blocks - edges), HDIM, 0))
    grads = lax.all_to_all(grads, group, 0, 0, tiled=True)
    column, grads = lax.optimization_barrier((column.astype(bf16), grads))
    parts = lax.all_to_all(column, ("half", "pair"), 0, 0, tiled=True)
    w_grad = jnp.sum(parts.astype(f32), axis=0)

    flat = shape((rows, width), bf16)
    output = call(
        output_kernel,
        "output",
        flat,
        vmem(2),
        flops=2 * rows * width * width,
        touched=2 * width * width,
        args=(attn, w_out),
    )
    d_queries, d_keys, d_values = call(
        split_kernel, "split", (flat,) * 3, vmem(1), args=(grads,)
    )
    return (output[None], d_queries[None], d_keys[None], d_values[None], w_grad)


def solution(mesh):
    ctx_count, dp_count = mesh.devices.shape
    pairs = ctx_count // (HALVES * CORES)
    fine = Mesh(
        mesh.devices.reshape(HALVES, pairs, CORES, dp_count), ("half", "pair", "core", "dp")
    )
    ctx = ("half", "pair", "core")
    tokens = P("dp", ctx, None)
    return jax.shard_map(
        per_device,
        mesh=fine,
        in_specs=(tokens, tokens, tokens, P(), tokens, P("dp", None)),
        out_specs=(tokens, tokens, tokens, tokens, P(ctx + ("dp",), None)),
        check_vma=False,
    )
```
